512 devices in a mesh: dom: 64 (over x, z), feat: 8 (over y, core).
Axes of the slice: x: 4, y: 4, z: 16, core: 2. Of those that a mesh axis runs over, the one named last changes fastest.
Arguments:
- node_feats: float32 [512, 131072], P('feat', 'dom'), may hold values from -6 to 6
- weight: float32 [512, 512], replicated, may hold values from -0.25 to 0.25
- tiles: float32 [1024, 4, 128, 128], P('dom'), may hold values from -0.25 to 0.25
- block_cols: int32 [1024, 4], P('dom'), may hold values from 0 to 47, as said below
- block_count: int32 [1024], P('dom'), may hold values from 2 to 4, as said below
- hub_ids: int32 [1024], replicated, may hold values from 0 to 131071, as said below
- hub_adj: float32 [1024, 131072], P(None, 'dom'), may hold values from -0.0234375 to 0.0234375
- cotangent: float32 [512, 131072], P('feat', 'dom'), may hold values from -6 to 6
Outputs:
- activated: float32 [512, 131072], P('feat', 'dom')
- feat_grad: float32 [512, 131072], P('feat', 'dom')
- weight_grad: float32 [512, 512], P('dom', 'feat')
The draws below stay inside these ranges and needn't reach their ends.
Inputs may be any that keep to these rules, and one draw needn't show every extreme that they name: `block_count`: every row block uses 2 to 4 slots, and some row block uses all 4. `block_cols`: in every row block, slot 0 names a block of the previous index of dom (below 16) and slot 1 a block of the next index of dom (32 or more); further slots name any of the three. `hub_ids`: hub ids are distinct. The vertices of one index of dom (2048 of them) contain at most 64 hubs, and in every draw some index of dom contains exactly 64.
All inputs are finite; a program needn't handle non-finite values.
Results may differ from the reference program's by a relative error of at most 0.000084.
Values sent between devices are 32-bit elements; how exact they have to be, the bound alone decides.
A program may use at most 128 MiB of HBM per device.

```python
import math
import jax
import jax.numpy as jnp
from jax import lax

F = 512
NB_DEV = 16
K_MOST = 4
HUB_DEV = 16
HUB_MOST = 64
NHUB = 1024
NBLK = 1024
NV = 131072
N_DOM = 64


def draw_block_cols(key, part):
    key = jax.random.fold_in(key, 31)
    key_lower, key_upper, key_rest = jax.random.split(key, 3)
    lower = jax.random.randint(key_lower, (NBLK, 1), 0, NB_DEV)
    upper = jax.random.randint(key_upper, (NBLK, 1), 2 * NB_DEV, 3 * NB_DEV)
    rest = jax.random.randint(key_rest, (NBLK, K_MOST - 2), 0, 3 * NB_DEV)
    return jnp.concatenate([lower, upper, rest], axis=1).astype(jnp.int32)


def draw_block_count(key, part):
    key = jax.random.fold_in(key, 11)
    first, second = jax.random.split(key)
    counts = jax.random.randint(first, (NBLK,), 2, K_MOST + 1)
    full_at = jax.random.randint(second, (), 0, NBLK)
    counts = jnp.where(jnp.arange(NBLK) == full_at, K_MOST, counts)
    return counts.astype(jnp.int32)


def draw_hub_ids(key, part):
    key = jax.random.fold_in(key, 23)
    key_order, key_group, key_local, key_shuffle = jax.random.split(key, 4)
    order = jax.random.permutation(key_order, N_DOM).astype(jnp.int32)
    last_dev = N_DOM - 1
    where_last = jnp.argmax(order == last_dev)
    first_dev = order[0]
    order = order.at[where_last].set(first_dev).at[0].set(last_dev)
    where_one = jnp.argmax(order == 1)
    fourth_dev = order[4]
    order = order.at[where_one].set(fourth_dev).at[4].set(1)
    heavy = jax.random.randint(key_group, (N_DOM // 4,), 0, 2)
    heavy = jnp.where(jnp.arange(N_DOM // 4) == 0, 1, heavy)
    heavy = jnp.where(jnp.arange(N_DOM // 4) == 1, 0, heavy)
    place = jnp.arange(N_DOM)
    within = place % 4
    counts_at = jnp.where(heavy[place // 4] == 1, jnp.where(within == 0, HUB_MOST, 0), HUB_DEV)
    device_counts = jnp.zeros((N_DOM,), jnp.int32).at[order].set(counts_at.astype(jnp.int32))
    count_zero = device_counts[0]
    count_one = device_counts[1]
    device_counts = device_counts.at[0].set(count_one).at[1].set(count_zero)
    owners = jnp.repeat(jnp.arange(N_DOM, dtype=jnp.int32), device_counts, total_repeat_length=NHUB)
    starts = jnp.cumsum(device_counts) - device_counts
    rank = jnp.arange(NHUB, dtype=jnp.int32) - starts[owners]
    rows_dev = NB_DEV * 128
    keys = jax.random.split(key_local, N_DOM)
    locals_all = jax.vmap(lambda one: jax.random.permutation(one, rows_dev))(keys).astype(jnp.int32)
    last_perm = locals_all[last_dev]
    where_top = jnp.argmax(last_perm == rows_dev - 1)
    first_local = last_perm[0]
    last_perm = last_perm.at[where_top].set(first_local).at[0].set(rows_dev - 1)
    locals_all = locals_all.at[last_dev].set(last_perm)
    zero_perm = locals_all[0]
    where_bottom = jnp.argmax(zero_perm == 0)
    head_local = zero_perm[0]
    zero_perm = zero_perm.at[where_bottom].set(head_local).at[0].set(0)
    locals_all = locals_all.at[0].set(zero_perm)
    vertex = owners * rows_dev + locals_all[owners, rank]
    shuffle = jax.random.permutation(key_shuffle, NHUB)
    return vertex[shuffle].astype(jnp.int32)


def block_levels(own_key, extent, cuts, low, top_value):
    def one(axis_at, blocks):
        steps = jax.random.uniform(jax.random.fold_in(jax.random.fold_in(own_key, 6), axis_at), (blocks,), jnp.float32, low / len(cuts), top_value / len(cuts))
        return jnp.repeat(jnp.exp(steps), extent[axis_at] // blocks).reshape((-1,) + (1,) * (len(extent) - axis_at - 1))

    level = one(*cuts[0])
    for cut in cuts[1:]:
        level = level * one(*cut)
    return level


def gaussian(rng, shape, deviation, limit, pieces=(), held_as=jnp.bfloat16):
    array = deviation * jax.random.normal(rng, shape, jnp.float32)
    if pieces:
        array = array * block_levels(rng, shape, pieces, -0.22, 0.18)
    return jnp.clip(array, -limit, limit).astype(held_as)


def setup_inputs(seed: int = 0) -> dict:
    key_list = jax.random.split(jax.random.key(seed), 9)
    return {
        "node_feats": gaussian(key_list[0], (F, NV), 1.0, 6.0, ((0, 8), (1, 64)), jnp.float32),
        "weight": gaussian(key_list[1], (F, F), F ** -0.5, 0.25, (), jnp.float32),
        "tiles": gaussian(key_list[2], (NBLK, K_MOST, 128, 128), (128 * K_MOST) ** -0.5, 0.25, ((0, 64),), jnp.float32),
        "block_cols": draw_block_cols(jax.random.fold_in(key_list[8], 71), 0),
        "block_count": draw_block_count(jax.random.fold_in(key_list[8], 71), 0),
        "hub_ids": draw_hub_ids(jax.random.fold_in(key_list[8], 71), 0),
        "hub_adj": gaussian(key_list[6], (NHUB, NV), (NHUB * N_DOM) ** -0.5, 0.0234375, ((1, 64),), jnp.float32),
        "cotangent": gaussian(key_list[7], (F, NV), 1.0, 6.0, ((0, 8), (1, 64)), jnp.float32),
    }


def reference(node_feats, weight, tiles, block_cols, block_count, hub_ids, hub_adj, cotangent):
    highest = lax.Precision.HIGHEST
    width = node_feats.shape[0]
    total = node_feats.shape[1]
    nblk = total // 128
    slots = block_cols.shape[1]
    proj = jnp.dot(weight.T, node_feats, precision=highest, preferred_element_type=jnp.float32)
    base_block = (jnp.arange(nblk, dtype=jnp.int32) // NB_DEV - 1) * NB_DEV
    global_cols = ((base_block[:, None] + block_cols) % nblk).astype(jnp.int32)
    live = (jnp.arange(slots, dtype=jnp.int32)[None, :] < block_count[:, None]).astype(jnp.float32)
    blocks = proj.reshape(width, nblk, 128)
    picked = jnp.take(blocks, global_cols, axis=1) * live[None, :, :, None]
    agg = jnp.einsum('fbkc,bkrc->fbr', picked, tiles, precision=highest).reshape(width, total)
    agg = agg + jnp.dot(jnp.take(proj, hub_ids, axis=1), hub_adj, precision=highest, preferred_element_type=jnp.float32)
    sig = jax.nn.sigmoid(agg)
    activated = agg * sig
    grad_agg = cotangent * sig * (1.0 + agg * (1.0 - sig))
    contrib = jnp.einsum('fbr,bkrc->fbkc', grad_agg.reshape(width, nblk, 128), tiles, precision=highest)
    contrib = contrib * live[None, :, :, None]
    grad_blocks = jnp.zeros((width, nblk, 128), jnp.float32).at[:, global_cols.reshape(-1)].add(contrib.reshape(width, nblk * slots, 128))
    grad_proj = grad_blocks.reshape(width, total)
    hub_part = lax.dot_general(grad_agg, hub_adj, (((1,), (1,)), ((), ())), precision=highest)
    grad_proj = grad_proj.at[:, hub_ids].add(hub_part)
    feat_grad = jnp.dot(weight, grad_proj, precision=highest, preferred_element_type=jnp.float32)
    weight_grad = lax.dot_general(node_feats, grad_proj, (((1,), (1,)), ((), ())), precision=highest) / math.sqrt(total)
    return (activated, feat_grad, weight_grad)
```

```python
import functools
import math

import jax
import jax.numpy as jnp
from jax import lax
from jax.experimental import pallas as pl
from jax.experimental.pallas import tpu as pltpu
from jax.sharding import PartitionSpec as P

MESH = pl.DeviceIdType.MESH
F32 = jnp.float32
BF16 = jnp.bfloat16
NN = (((1,), (0,)), ((), ()))
NT = (((1,), (1,)), ((), ()))


def split(value):
    high = value.astype(BF16)
    low = (value - high.astype(F32)).astype(BF16)
    return high, low


def mm(a, b, dims):
    return lax.dot_general(a, b, dims, preferred_element_type=F32)


def stacked(value):
    high, low = split(value)
    return jnp.concatenate([high, low], axis=0)


def mm3(left, right_high, right_low, dims):
    rows = left.shape[0] // 2
    both = mm(left, right_high, dims)
    return both[:rows] + both[rows:] + mm(left[:rows], right_low, dims)


def kernel(
    sizes,
    x, w, tiles, hub_adj, cot, ids, cols, live, ent, keep, last, has,
    act, fg, wg,
    ext, adj_f32, adj_hi, adj_lo, tiles_f32, cat_hi, cat_lo, pick,
    w_f32, w_st, wt_st, y_send, y_all, cot_all, act_send, q_send, q_all,
    hub_acc, hub_in, contrib, runs, b_send, b_recv, fg_out,
    h_src, h_rx, h_zsrc, h_rz, h_zg, h_xg,
    wg_src, wg_recv, wg_xsrc, wg_rx, wg_zsrc, wg_rz,
    s_x, s_misc, s_adj, s_cot_own, s_out,
    s_nbr, s_cot, s_y, s_q, s_act, s_back, s_hx, s_hz, s_hzg, s_hxg, s_wf, s_wx, s_wz,
):
    nx, nz, nf, nb, slots = sizes
    nd = nx * nz
    fl, vl = x.shape
    full = w.shape[0]
    nh = hub_adj.shape[0]
    pb = nb // nf
    vw = pb * 128
    row_tiles = fl // 8
    per_q = nh // 128 // nx
    dom = lax.axis_index("dom")
    me = lax.axis_index("feat")
    my_x, my_z = dom // nz, dom % nz
    nxt, prv = (dom + 1) % nd, (dom + nd - 1) % nd

    def feat_peer(k):
        return (me + k) % nf

    def feat_from(k):
        return (me + nf - k) % nf

    def x_peer(k):
        return (my_x + k) % nx

    def z_peer(k):
        return (my_z + k) % nz

    def z_from(k):
        return (my_z + nz - k) % nz

    def to(domain, feature):
        return {"dom": domain, "feat": feature}

    def x_dev(k):
        return to(x_peer(k) * nz + my_z, me)

    def z_dev(k):
        return to(my_x * nz + z_peer(k), me)

    def f_dev(k):
        return to(dom, feat_peer(k))

    def remote(src, dst, sems, at, device):
        return pltpu.make_async_remote_copy(
            src_ref=src, dst_ref=dst, send_sem=sems.at[0, at], recv_sem=sems.at[1, at],
            device_id=device, device_id_type=MESH,
        )

    def loop(lower, upper, body):
        def step(i, carry):
            body(i)
            return carry

        lax.fori_loop(lower, upper, step, 0)

    x_loads = [
        pltpu.make_async_copy(x.at[:, pl.ds(128 * b, 128)], ext.at[nb + b], s_x.at[b])
        for b in range(nb)
    ]
    for copy in x_loads:
        copy.start()
    tiles_load = pltpu.make_async_copy(tiles, tiles_f32, s_misc.at[0])
    w_load = pltpu.make_async_copy(w, w_f32, s_misc.at[1])
    adj_loads = [
        pltpu.make_async_copy(hub_adj.at[:, pl.ds(vw * p, vw)], adj_f32.at[p], s_adj.at[p])
        for p in range(nf)
    ]
    cot_own = pltpu.make_async_copy(
        cot.at[:, pl.ds(pl.multiple_of(vw * me, 128), vw)],
        cot_all.at[pl.ds(pl.multiple_of(fl * me, 8), fl), :], s_cot_own,
    )
    tiles_load.start()
    w_load.start()
    cot_own.start()
    for copy in adj_loads:
        copy.start()

    barrier = pltpu.get_barrier_semaphore()

    def greet(device):
        pl.semaphore_signal(barrier, inc=1, device_id=device, device_id_type=MESH)

    greet(to(nxt, me))
    greet(to(prv, me))
    for k in range(1, nx):
        greet(x_dev(k))
    loop(1, nz, lambda k: greet(z_dev(k)))
    loop(1, nf, lambda k: greet(f_dev(k)))
    pl.semaphore_wait(barrier, 2 + (nx - 1) + (nz - 1) + (nf - 1))

    for copy in x_loads:
        copy.wait()
    mine = ext.at[pl.ds(nb, nb)]
    to_nxt = remote(mine, ext.at[pl.ds(0, nb)], s_nbr, 0, to(nxt, me))
    to_prv = remote(mine, ext.at[pl.ds(2 * nb, nb)], s_nbr, 1, to(prv, me))
    to_nxt.start()
    to_prv.start()

    def cot_copy(k):
        p = feat_peer(k)
        return remote(
            cot.at[:, pl.ds(pl.multiple_of(vw * p, 128), vw)],
            cot_all.at[pl.ds(pl.multiple_of(fl * me, 8), fl), :], s_cot, k - 1, f_dev(k),
        )

    local_id = ids[...] - dom * vl
    hub_acc[...] = jnp.zeros_like(hub_acc)

    def own_hubs(p):
        row = lax.broadcasted_iota(jnp.int32, (vw, nh), 0) + p * vw
        chunk = jnp.where(row == local_id, 1.0, 0.0).astype(BF16)
        pick[p] = chunk
        left = stacked(jnp.concatenate([ext[nb + pb * p + j] for j in range(pb)], axis=1))
        both = mm(left, chunk, NN)
        hub_acc[...] += both[:fl] + both[fl:]

    loop(0, nf, own_hubs)

    def x_rs_copy(s, k):
        return remote(h_src.at[s, x_peer(k)], h_rx.at[s, k - 1], s_hx.at[s], k - 1, x_dev(k))

    def z_rs_copy(s, k):
        return remote(h_zsrc.at[s, z_peer(k)], h_rz.at[s, k - 1], s_hz.at[s], k - 1, z_dev(k))

    def z_ag_copy(s, k):
        return remote(h_zg.at[s, my_z], h_zg.at[s, my_z], s_hzg.at[s], k - 1, z_dev(k))

    def z_ag_recv(s, k):
        at = h_zg.at[s, z_from(k)]
        return remote(at, at, s_hzg.at[s], k - 1, z_dev(k))

    def x_ag_copy(s, k):
        return remote(h_zg.at[s], h_xg.at[s, my_x], s_hxg.at[s], k - 1, x_dev(k))

    def x_ag_recv(s, k):
        return remote(
            h_zg.at[s], h_xg.at[s, (my_x + nx - k) % nx], s_hxg.at[s], k - 1, x_dev(k)
        )

    def hub_start(s):
        for q in range(nx):
            for i in range(nz):
                r, c = i // per_q, q * per_q + i % per_q
                h_src[s, q, i] = hub_acc[8 * r : 8 * r + 8, 128 * c : 128 * c + 128]
        for k in range(1, nx):
            x_rs_copy(s, k).start()

    def hub_z(s):
        for k in range(1, nx):
            x_rs_copy(s, k).wait_recv()
        total = h_src[s, my_x]
        for k in range(1, nx):
            total += h_rx[s, k - 1]
        h_zsrc[s] = total
        loop(1, nz, lambda k: z_rs_copy(s, k).start())

    def hub_zg(s):
        loop(1, nz, lambda k: z_rs_copy(s, k).wait_recv())
        total = h_zsrc[s, my_z]
        for k in range(1, nz):
            total += h_rz[s, k - 1]
        h_zg[s, my_z] = total
        loop(1, nz, lambda k: z_ag_copy(s, k).start())

    def hub_xg(s):
        loop(1, nz, lambda k: z_ag_recv(s, k).wait_recv())
        for k in range(1, nx):
            x_ag_copy(s, k).start()
        h_xg[s, my_x] = h_zg[s]

    def hub_end(s):
        for k in range(1, nx):
            x_ag_recv(s, k).wait_recv()
        for q in range(nx):
            for i in range(nz):
                r, c = i // per_q, q * per_q + i % per_q
                high, low = split(h_xg[s, q, i])
                hub_acc[8 * r : 8 * r + 8, 128 * c : 128 * c + 128] = h_xg[s, q, i]
        hub_in[...] = stacked(hub_acc[...])

    hub_start(0)
    loop(1, nf, lambda k: cot_copy(k).start())

    tiles_load.wait()

    def split_tiles(b):
        both = [split(tiles_f32[b, k]) for k in range(slots)]
        cat_hi[b] = jnp.concatenate([one[0] for one in both], axis=1)
        cat_lo[b] = jnp.concatenate([one[1] for one in both], axis=1)

    loop(0, nb, split_tiles)
    hub_z(0)

    w_load.wait()
    w_st[...] = stacked(w_f32[...])
    wt_st[...] = stacked(w_f32[...].T)

    def split_adj(p):
        high, low = split(adj_f32[p])
        adj_hi[p] = high
        adj_lo[p] = low

    for copy in adj_loads:
        copy.wait()
    loop(0, nf // 2, split_adj)
    hub_zg(0)
    loop(nf // 2, nf, split_adj)
    hub_xg(0)

    to_nxt.wait_recv()
    to_prv.wait_recv()

    def tile_part(p):
        for j in range(pb):
            b = p * pb + j
            left = jnp.concatenate(
                [ext[cols[b * slots + k]] * live[b * slots + k] for k in range(slots)], axis=1
            )
            y_send[p, :, 128 * j : 128 * j + 128] = mm3(stacked(left), cat_hi[b], cat_lo[b], NT)

    loop(0, nf, tile_part)
    hub_end(0)

    def y_copy(k):
        return remote(
            y_send.at[feat_peer(k)], y_all.at[pl.ds(pl.multiple_of(fl * me, 8), fl), :],
            s_y, k - 1, f_dev(k),
        )

    def y_recv(k):
        at = y_all.at[pl.ds(pl.multiple_of(fl * feat_from(k), 8), fl), :]
        return remote(y_send.at[0], at, s_y, k - 1, f_dev(k))

    def hub_to_y(p):
        return y_send[p] + mm3(hub_in[...], adj_hi[p], adj_lo[p], NN)

    def hub_part(k):
        p = feat_peer(k)
        y_send[p] = hub_to_y(p)
        y_copy(k).start()

    loop(1, nf, hub_part)
    y_all[pl.ds(pl.multiple_of(fl * me, 8), fl), :] = hub_to_y(me)

    loop(1, nf, lambda k: y_recv(k).wait_recv())
    y_hi, y_lo = split(y_all[...])
    agg = mm3(wt_st[...], y_hi, y_lo, NN)
    sig = 1.0 / (1.0 + jnp.exp(-agg))
    act_send[...] = agg * sig
    cot_own.wait()

    def cot_recv(k):
        at = cot_all.at[pl.ds(pl.multiple_of(fl * feat_from(k), 8), fl), :]
        return remote(cot.at[:, pl.ds(0, vw)], at, s_cot, k - 1, f_dev(k))

    loop(1, nf, lambda k: cot_recv(k).wait_recv())
    grad = cot_all[...] * sig * (1.0 + agg * (1.0 - sig))
    g_hi, g_lo = split(grad)
    q_send[...] = mm3(w_st[...], g_hi, g_lo, NN)

    def rows_of(ref, p):
        return ref.at[pl.ds(pl.multiple_of(fl * p, 8), fl), :]

    def q_copy(k):
        return remote(rows_of(q_send, feat_peer(k)), q_all.at[me], s_q, k - 1, f_dev(k))

    def q_recv(k):
        return remote(rows_of(q_send, me), q_all.at[feat_from(k)], s_q, k - 1, f_dev(k))

    loop(1, nf, lambda k: q_copy(k).start())
    q_all[me] = q_send[pl.ds(pl.multiple_of(fl * me, 8), fl), :]

    g_st = jnp.concatenate([g_hi, g_lo], axis=0)
    terms = mm3(g_st, y_hi, y_lo, NT)
    for p in range(nf):
        wg_src[p] = terms[fl * p : fl * p + fl]

    def wf_copy(k):
        return remote(wg_src.at[feat_peer(k)], wg_recv.at[k - 1], s_wf, k - 1, f_dev(k))

    loop(1, nf, lambda k: wf_copy(k).start())

    def act_at(p):
        return act.at[:, pl.ds(pl.multiple_of(vw * p, 128), vw)]

    def act_copy(k):
        return remote(rows_of(act_send, feat_peer(k)), act_at(me), s_act, k - 1, f_dev(k))

    def act_recv(k):
        return remote(rows_of(act_send, me), act_at(feat_from(k)), s_act, k - 1, f_dev(k))

    loop(1, nf, lambda k: act_copy(k).start())
    act_own = pltpu.make_async_copy(rows_of(act_send, me), act_at(me), s_misc.at[2])
    act_own.start()

    def hub_back(p):
        left = stacked(q_all[p])
        return mm3(left, adj_hi[p], adj_lo[p], NT)

    hub_acc[...] = hub_back(me)

    def hub_step(k):
        q_recv(k).wait_recv()
        hub_acc[...] += hub_back(feat_from(k))

    loop(1, nf, hub_step)
    hub_start(1)

    def slot_terms(p):
        for j in range(pb):
            b = p * pb + j
            left = stacked(q_all[p, :, 128 * j : 128 * j + 128])
            out = mm3(left, cat_hi[b], cat_lo[b], NN)
            for k in range(slots):
                contrib[b * slots + k] = out[:, 128 * k : 128 * k + 128]

    loop(0, nf, slot_terms)

    def run_step(j, total):
        total = total * keep[j] + contrib[ent[j]]
        runs[j] = total
        return total

    lax.fori_loop(0, nb * slots, run_step, jnp.zeros((fl, 128), F32))

    def back_send(b):
        b_send[0, b] = runs[last[b]] * has[b]
        b_send[1, b] = runs[last[2 * nb + b]] * has[2 * nb + b]

    loop(0, nb, back_send)
    back_prv = remote(b_send.at[0], b_recv.at[0], s_back, 0, to(prv, me))
    back_nxt = remote(b_send.at[1], b_recv.at[1], s_back, 1, to(nxt, me))
    back_prv.start()
    back_nxt.start()

    hub_z(1)
    hub_zg(1)

    loop(1, nf, lambda k: wf_copy(k).wait_recv())
    term = wg_src[me]
    for k in range(1, nf):
        term += wg_recv[k - 1]
    part = full // nx
    for q in range(nx):
        wg_xsrc[q] = term[:, part * q : part * q + part]

    def wx_copy(k):
        return remote(wg_xsrc.at[x_peer(k)], wg_rx.at[k - 1], s_wx, k - 1, x_dev(k))

    for k in range(1, nx):
        wx_copy(k).start()

    hub_xg(1)

    for k in range(1, nx):
        wx_copy(k).wait_recv()
    term = wg_xsrc[my_x]
    for k in range(1, nx):
        term += wg_rx[k - 1]
    term = term.T
    lanes = wg_zsrc.shape[2]
    if lanes > fl:
        term = jnp.concatenate([term, jnp.zeros((part, lanes - fl), F32)], axis=1)
    wg_zsrc[...] = term.reshape(wg_zsrc.shape)

    def wz_copy(k):
        return remote(wg_zsrc.at[z_peer(k)], wg_rz.at[k - 1], s_wz, k - 1, z_dev(k))

    loop(1, nz, lambda k: wz_copy(k).start())

    hub_end(1)
    back_prv.wait_recv()
    back_nxt.wait_recv()

    def out_copy(p):
        return pltpu.make_async_copy(
            fg_out.at[p], fg.at[:, pl.ds(pl.multiple_of(vw * p, 128), vw)], s_out.at[p]
        )

    def finish(p):
        both = mm(hub_in[...], pick[p], NT)
        placed = both[:fl] + both[fl:]
        for j in range(pb):
            b = p * pb + j
            own = runs[last[nb + b]] * has[nb + b]
            total = placed[:, 128 * j : 128 * j + 128] + own + b_recv[0, b] + b_recv[1, b]
            fg_out[p, :, 128 * j : 128 * j + 128] = total
        out_copy(p).start()

    loop(0, nf, finish)

    loop(1, nz, lambda k: wz_copy(k).wait_recv())
    term = wg_zsrc[my_z]
    for k in range(1, nz):
        term += wg_rz[k - 1]
    wg[...] = term[:, :fl] * (1.0 / math.sqrt(vl * nd))

    act_own.wait()
    loop(1, nf, lambda k: act_recv(k).wait_recv())
    to_nxt.wait_send()
    to_prv.wait_send()
    back_prv.wait_send()
    back_nxt.wait_send()

    def feat_sent(k):
        cot_copy(k).wait_send()
        y_copy(k).wait_send()
        q_copy(k).wait_send()
        wf_copy(k).wait_send()
        act_copy(k).wait_send()

    loop(1, nf, feat_sent)
    for k in range(1, nx):
        for s in range(2):
            x_rs_copy(s, k).wait_send()
            x_ag_copy(s, k).wait_send()
        wx_copy(k).wait_send()

    def z_sent(k):
        for s in range(2):
            z_rs_copy(s, k).wait_send()
            z_ag_copy(s, k).wait_send()
        wz_copy(k).wait_send()

    loop(1, nz, z_sent)
    loop(0, nf, lambda p: out_copy(p).wait())


def local(nd, nf, nx, node_feats, weight, tiles, block_cols, block_count, hub_ids, hub_adj, cotangent):
    nz = nd // nx
    fl, vl = node_feats.shape
    full = weight.shape[0]
    nb, slots = block_cols.shape
    nh = hub_adj.shape[0]
    vw = vl // nf
    entries = nb * slots

    col = block_cols.reshape(-1)
    alive = (jnp.arange(slots, dtype=jnp.int32)[None, :] < block_count[:, None]).reshape(-1)
    target = jnp.where(alive, col, 3 * nb)
    at = jnp.arange(entries, dtype=jnp.int32)
    before = target[None, :] * entries + at[None, :] < target[:, None] * entries + at[:, None]
    rank = jnp.sum(before.astype(jnp.int32), axis=1)
    placed = rank[:, None] == at[None, :]
    ent = jnp.sum(jnp.where(placed, at[:, None], 0), axis=0)
    repeat = jnp.any((target[None, :] == target[:, None]) & (at[None, :] < at[:, None]), axis=1)
    keep = jnp.sum(jnp.where(placed & repeat[:, None], 1.0, 0.0), axis=0)
    blocks = jnp.arange(3 * nb, dtype=jnp.int32)
    upto = jnp.sum((target[:, None] <= blocks[None, :]).astype(jnp.int32), axis=0)
    last = jnp.maximum(upto - 1, 0)
    has = jnp.any(target[:, None] == blocks[None, :], axis=0).astype(F32)
    live = alive.astype(F32)

    lanes = max(fl, 128)
    vm = pltpu.VMEM
    dma = pltpu.SemaphoreType.DMA
    hub_tile = (8, 128)
    scratch = [
        vm((3 * nb, fl, 128), F32),
        vm((nf, nh, vw), F32), vm((nf, nh, vw), BF16), vm((nf, nh, vw), BF16),
        vm((nb, slots, 128, 128), F32),
        vm((nb, 128, slots * 128), BF16), vm((nb, 128, slots * 128), BF16),
        vm((nf, vw, nh), BF16),
        vm((full, full), F32), vm((2 * full, full), BF16), vm((2 * full, full), BF16),
        vm((nf, fl, vw), F32), vm((full, vw), F32), vm((full, vw), F32), vm((full, vw), F32),
        vm((full, vw), F32), vm((nf, fl, vw), F32),
        vm((fl, nh), F32), vm((2 * fl, nh), BF16),
        vm((entries, fl, 128), F32), vm((entries, fl, 128), F32),
        vm((2, nb, fl, 128), F32), vm((2, nb, fl, 128), F32), vm((nf, fl, vw), F32),
        vm((2, nx, nz) + hub_tile, F32), vm((2, nx - 1, nz) + hub_tile, F32),
        vm((2, nz) + hub_tile, F32), vm((2, nz - 1) + hub_tile, F32),
        vm((2, nz) + hub_tile, F32), vm((2, nx, nz) + hub_tile, F32),
        vm((nf, fl, full), F32), vm((nf - 1, fl, full), F32),
        vm((nx, fl, full // nx), F32), vm((nx - 1, fl, full // nx), F32),
        vm((nz, full // nx // nz, lanes), F32), vm((nz - 1, full // nx // nz, lanes), F32),
        dma((nb,)), dma((3,)), dma((nf,)), dma, dma((nf,)),
        dma((2, 2)), dma((2, nf - 1)), dma((2, nf - 1)), dma((2, nf - 1)), dma((2, nf - 1)),
        dma((2, 2)),
        dma((2, 2, nx - 1)), dma((2, 2, nz - 1)), dma((2, 2, nz - 1)), dma((2, 2, nx - 1)),
        dma((2, nf - 1)), dma((2, nx - 1)), dma((2, nz - 1)),
    ]
    hbm = pl.BlockSpec(memory_space=pl.ANY)
    vmem = pl.BlockSpec(memory_space=pltpu.VMEM)
    smem = pl.BlockSpec(memory_space=pltpu.SMEM)
    return pl.pallas_call(
        functools.partial(kernel, (nx, nz, nf, nb, slots)),
        out_shape=(
            jax.ShapeDtypeStruct((fl, vl), F32),
            jax.ShapeDtypeStruct((fl, vl), F32),
            jax.ShapeDtypeStruct((full // nd, fl), F32),
        ),
        in_specs=[hbm] * 5 + [vmem] + [smem] * 6,
        out_specs=(hbm, hbm, vmem),
        scratch_shapes=scratch,
        compiler_params=pltpu.CompilerParams(
            collective_id=0, has_side_effects=True, vmem_limit_bytes=60 * 1024 * 1024
        ),
    )(
        node_feats, weight, tiles, hub_adj, cotangent, hub_ids.reshape(1, nh),
        col, live, ent, keep, last, has,
    )


def solution(mesh):
    nd, nf = mesh.shape["dom"], mesh.shape["feat"]
    nx = 4 if nd == 64 else 2
    return jax.shard_map(
        functools.partial(local, nd, nf, nx),
        mesh=mesh,
        in_specs=(
            P("feat", "dom"),
            P(),
            P("dom", None, None, None),
            P("dom", None),
            P("dom"),
            P(),
            P(None, "dom"),
            P("feat", "dom"),
        ),
        out_specs=(P("feat", "dom"), P("feat", "dom"), P("dom", "feat")),
        check_vma=False,
    )
```

```python
import functools
import math

import jax
import jax.numpy as jnp
from jax import lax
from jax.experimental import pallas as pl
from jax.experimental.pallas import tpu as pltpu
from jax.sharding import PartitionSpec as P

MESH = pl.DeviceIdType.MESH
F32 = jnp.float32
BF16 = jnp.bfloat16
NN = (((1,), (0,)), ((), ()))
NT = (((1,), (1,)), ((), ()))


def split(value):
    high = value.astype(BF16)
    low = (value - high.astype(F32)).astype(BF16)
    return high, low


def mm(a, b, dims):
    return lax.dot_general(a, b, dims, preferred_element_type=F32)


def stacked(value):
    high, low = split(value)
    return jnp.concatenate([high, low], axis=0)


def mm3(left, right_high, right_low, dims):
    rows = left.shape[0] // 2
    both = mm(left, right_high, dims)
    return both[:rows] + both[rows:] + mm(left[:rows], right_low, dims)


def kernel(
    sizes, groups,
    x, w, tiles, hub_adj, cot, ids, cols_v, cols, count,
    act, fg, wg,
    ext, adj_f32, adj_hi, adj_lo, tiles_f32, cat_hi, cat_lo, pick,
    w_f32, w_st, wt_st, y_send, y_all, cot_all, act_send, q_send, q_all,
    hub_acc, hub_in, contrib, runs, b_send, b_recv, fg_out, order_v, order,
    h_src, h_rx, h_zsrc, h_rz, h_zg, h_xg,
    wg_src, wg_pair, wg_half, wg_recv, wg_xsrc, wg_rx, wg_zsrc, wg_rz,
    s_x, s_misc, s_adj, s_cot_own, s_out,
    s_nbr, s_cot, s_y, s_q, s_act, s_back, s_hx, s_hz, s_hzg, s_hxg, s_wp, s_wf, s_wx, s_wz,
):
    nx, nz, nf, nb, slots = sizes
    far, z_first, z_near = groups
    ny = nf // 2
    nd = nx * nz
    fl, vl = x.shape
    full = w.shape[0]
    nh = hub_adj.shape[0]
    pb = nb // nf
    vw = pb * 128
    row_tiles = fl // 8
    per_q = nh // 128 // nx
    dom = lax.axis_index("dom")
    me = lax.axis_index("feat")
    my_x, my_z = dom // nz, dom % nz
    my_y, my_core = me // 2, me % 2
    nxt, prv = (dom + 1) % nd, (dom + nd - 1) % nd

    def feat_peer(k):
        return (me + k) % nf

    def feat_from(k):
        return (me + nf - k) % nf

    def x_peer(k):
        return (my_x + k) % nx

    def z_peer(k):
        return (my_z + k) % nz

    def z_from(k):
        return (my_z + nz - k) % nz

    def to(domain, feature):
        return {"dom": domain, "feat": feature}

    def x_dev(k):
        return to(x_peer(k) * nz + my_z, me)

    def z_dev(k):
        return to(my_x * nz + z_peer(k), me)

    def f_dev(k):
        return to(dom, feat_peer(k))

    def remote(src, dst, sems, at, device):
        return pltpu.make_async_remote_copy(
            src_ref=src, dst_ref=dst, send_sem=sems.at[0, at], recv_sem=sems.at[1, at],
            device_id=device, device_id_type=MESH,
        )

    def loop(lower, upper, body):
        def step(i, carry):
            body(i)
            return carry

        lax.fori_loop(lower, upper, step, 0)

    x_loads = [
        pltpu.make_async_copy(x.at[:, pl.ds(128 * b, 128)], ext.at[nb + b], s_x.at[b])
        for b in range(nb)
    ]
    for copy in x_loads:
        copy.start()
    tiles_load = pltpu.make_async_copy(tiles, tiles_f32, s_misc.at[0])
    w_load = pltpu.make_async_copy(w, w_f32, s_misc.at[1])
    adj_loads = [
        pltpu.make_async_copy(hub_adj.at[:, pl.ds(vw * p, vw)], adj_f32.at[p], s_adj.at[p])
        for p in range(nf)
    ]
    cot_own = pltpu.make_async_copy(
        cot.at[:, pl.ds(pl.multiple_of(vw * me, 128), vw)],
        cot_all.at[pl.ds(pl.multiple_of(fl * me, 8), fl), :], s_cot_own,
    )
    tiles_load.start()
    w_load.start()
    cot_own.start()
    for copy in adj_loads:
        copy.start()

    barrier = pltpu.get_barrier_semaphore()

    def greet(device):
        pl.semaphore_signal(barrier, inc=1, device_id=device, device_id_type=MESH)

    greet(to(nxt, me))
    greet(to(prv, me))
    for k in range(1, nx):
        greet(x_dev(k))
    loop(1, nz, lambda k: greet(z_dev(k)))
    loop(1, nf, lambda k: greet(f_dev(k)))
    for copy in x_loads:
        copy.wait()

    half = nb // 2

    def ext_copy(side, h):
        at, device = ((0, to(nxt, me)), (2 * nb, to(prv, me)))[side]
        return remote(
            ext.at[pl.ds(nb + half * h, half)], ext.at[pl.ds(at + half * h, half)],
            s_nbr.at[h], side, device,
        )

    def both_sides(copies, h):
        copies(0, h).start()
        copies(1, h).start()

    def cot_copy(k):
        p = feat_peer(k)
        return remote(
            cot.at[:, pl.ds(pl.multiple_of(vw * p, 128), vw)],
            cot_all.at[pl.ds(pl.multiple_of(fl * me, 8), fl), :], s_cot, k - 1, f_dev(k),
        )

    local_id = ids[...] - dom * vl
    hub_acc[...] = jnp.zeros_like(hub_acc)

    def own_hubs(p):
        row = lax.broadcasted_iota(jnp.int32, (vw, 128), 0) + p * vw
        chunk = jnp.concatenate(
            [
                jnp.where(row == local_id[g : g + 1], 1.0, 0.0).astype(BF16)
                for g in range(nh // 128)
            ],
            axis=1,
        )
        pick[p] = chunk
        left = stacked(jnp.concatenate([ext[nb + pb * p + j] for j in range(pb)], axis=1))
        both = mm(left, chunk, NN)
        hub_acc[...] += both[:fl] + both[fl:]

    loop(0, nf, own_hubs)

    pl.semaphore_wait(barrier, 2 + (nx - 1) + (nz - 1) + (nf - 1))

    parts = ((0, far), (far, nz - far))
    near = ((0, nz - far), (nz - far, far))
    far_steps = ((z_first, z_first + far),)
    near_steps = ((z_first + far, nz), (1, z_first))

    def steps(ranges, body):
        for lower, upper in ranges:
            loop(lower, upper, body)

    def x_rs_copy(s, k, h):
        at = pl.ds(*parts[h])
        return remote(
            h_src.at[s, x_peer(k), at], h_rx.at[s, k - 1, at], s_hx.at[s, h], k - 1, x_dev(k)
        )

    def z_rs_copy(s, k):
        src = h_zsrc.at[s, (k + nz - z_first) % nz]
        return remote(src, h_rz.at[s, k - 1], s_hz.at[s], k - 1, z_dev(k))

    def z_ag_copy(s, k):
        dst = h_zg.at[s, (z_near + nz - k) % nz]
        return remote(h_zg.at[s, z_near], dst, s_hzg.at[s], k - 1, z_dev(k))

    def x_ag_copy(s, k, h):
        at = pl.ds(*near[h])
        return remote(h_zg.at[s, at], h_xg.at[s, k, at], s_hxg.at[s, h], k - 1, x_dev(k))

    x_order = [2, 1, 3][:nx] if nx > 2 else [1]

    def hub_start(s):
        for q in range(nx):
            for i in range(nz):
                r, c = i // per_q, q * per_q + i % per_q
                at = (i + 2 * nz - my_z - z_first) % nz
                h_src[s, q, at] = hub_acc[8 * r : 8 * r + 8, 128 * c : 128 * c + 128]
        for h in range(2):
            for k in x_order:
                x_rs_copy(s, k, h).start()

    def hub_z(s):
        for h in range(2):
            for k in x_order:
                x_rs_copy(s, k, h).wait_recv()
            at = pl.ds(*parts[h])
            total = h_src[s, my_x, at]
            for k in range(1, nx):
                total += h_rx[s, k - 1, at]
            h_zsrc[s, at] = total
            steps((far_steps, near_steps)[h], lambda k: z_rs_copy(s, k).start())

    def hub_zg(s):
        loop(1, nz, lambda k: z_rs_copy(s, k).wait_recv())
        total = h_zsrc[s, nz - z_first]
        for k in range(1, nz):
            total += h_rz[s, k - 1]
        h_zg[s, z_near] = total
        steps(far_steps + near_steps, lambda k: z_ag_copy(s, k).start())

    def hub_xg(s, h):
        steps((near_steps, far_steps)[h], lambda k: z_ag_copy(s, k).wait_recv())
        for k in x_order:
            x_ag_copy(s, k, h).start()
        at = pl.ds(*near[h])
        h_xg[s, 0, at] = h_zg[s, at]

    def hub_end(s):
        for h in range(2):
            for k in x_order:
                x_ag_copy(s, k, h).wait_recv()
        for q in range(nx):
            for i in range(nz):
                r, c = i // per_q, q * per_q + i % per_q
                tile = h_xg[s, (my_x + nx - q) % nx, (i + nz - my_z + z_near) % nz]
                hub_acc[8 * r : 8 * r + 8, 128 * c : 128 * c + 128] = tile
        hub_in[...] = stacked(hub_acc[...])

    hub_start(0)
    tiles_load.wait()

    def split_tiles(b):
        both = [split(tiles_f32[b, k]) for k in range(slots)]
        cat_hi[b] = jnp.concatenate([one[0] for one in both], axis=1)
        cat_lo[b] = jnp.concatenate([one[1] for one in both], axis=1)

    loop(0, nb, split_tiles)
    hub_z(0)
    both_sides(ext_copy, 0)
    loop(1, nf, lambda k: cot_copy(k).start())

    entries = nb * slots
    none = 3 * nb
    row = lax.broadcasted_iota(jnp.int32, (nb, slots), 0)
    lane = lax.broadcasted_iota(jnp.int32, (nb, slots), 1)
    place = row * slots + lane
    counts = jnp.zeros((nb, slots), jnp.int32)
    for b in range(nb):
        counts = jnp.where(row == b, count[b], counts)
    target = jnp.where(lane < counts, cols_v[...], none)
    along = lax.broadcasted_iota(jnp.int32, (1, 128), 1)

    def one(flag):
        return jnp.where(flag, 1, 0)

    def rank_step(e, carry):
        rank, again, upto, found = carry
        b, k = e // slots, e % slots
        goal = jnp.where(k < count[b], cols[b, k], none)
        tie = one(target == goal) * one(place > e)
        return (
            rank + one(target > goal) + tie, jnp.maximum(again, tie),
            upto + one(along >= goal), jnp.maximum(found, one(along == goal)),
        )

    zero, zeros = jnp.zeros((nb, slots), jnp.int32), jnp.zeros((1, 128), jnp.int32)
    rank, again, upto, found = lax.fori_loop(0, entries, rank_step, (zero, zero, zeros, zeros))
    which, same = zeros, zeros
    for e in range(entries):
        b, k = e // slots, e % slots
        here = rank[b : b + 1, k : k + 1] == along
        which = jnp.where(here, e, which)
        same = jnp.where(here, again[b : b + 1, k : k + 1], same)
    order_v[0:1] = which
    order_v[1:2] = same
    order_v[2:3] = jnp.maximum(upto - 1, 0)
    order_v[3:4] = found
    order_copy = pltpu.make_async_copy(order_v, order, s_misc.at[2])
    order_copy.start()

    w_load.wait()
    w_st[...] = stacked(w_f32[...])
    wt_st[...] = stacked(w_f32[...].T)

    def split_adj(p):
        high, low = split(adj_f32[p])
        adj_hi[p] = high
        adj_lo[p] = low

    for copy in adj_loads:
        copy.wait()
    loop(0, nf // 2, split_adj)
    hub_zg(0)
    both_sides(ext_copy, 1)
    loop(nf // 2, nf, split_adj)
    order_copy.wait()
    hub_xg(0, 0)
    hub_xg(0, 1)

    for h in range(2):
        ext_copy(0, h).wait_recv()
        ext_copy(1, h).wait_recv()

    def tile_part(p):
        for j in range(pb):
            b = p * pb + j
            left = jnp.concatenate(
                [ext[cols[b, k]] * jnp.where(k < count[b], 1.0, 0.0) for k in range(slots)],
                axis=1,
            )
            y_send[p, :, 128 * j : 128 * j + 128] = mm3(stacked(left), cat_hi[b], cat_lo[b], NT)

    loop(0, nf, tile_part)
    hub_end(0)

    def y_copy(k):
        return remote(
            y_send.at[feat_peer(k)], y_all.at[pl.ds(pl.multiple_of(fl * me, 8), fl), :],
            s_y, k - 1, f_dev(k),
        )

    def y_recv(k):
        at = y_all.at[pl.ds(pl.multiple_of(fl * feat_from(k), 8), fl), :]
        return remote(y_send.at[0], at, s_y, k - 1, f_dev(k))

    def hub_to_y(p):
        return y_send[p] + mm3(hub_in[...], adj_hi[p], adj_lo[p], NN)

    def feat_order(i):
        return nf // 2 if nf < 4 else (nf // 2 + (1 - 2 * (i % 2)) * ((i + 1) // 2)) % nf

    def hub_part(i):
        k = feat_order(i)
        p = feat_peer(k)
        y_send[p] = hub_to_y(p)
        y_copy(k).start()

    loop(0, nf - 1, hub_part)
    y_all[pl.ds(pl.multiple_of(fl * me, 8), fl), :] = hub_to_y(me)

    loop(1, nf, lambda k: y_recv(k).wait_recv())
    y_hi, y_lo = split(y_all[...])
    agg = mm3(wt_st[...], y_hi, y_lo, NN)
    sig = 1.0 / (1.0 + jnp.exp(-agg))
    act_send[...] = agg * sig
    cot_own.wait()

    def cot_recv(k):
        at = cot_all.at[pl.ds(pl.multiple_of(fl * feat_from(k), 8), fl), :]
        return remote(cot.at[:, pl.ds(0, vw)], at, s_cot, k - 1, f_dev(k))

    loop(1, nf, lambda k: cot_recv(k).wait_recv())
    grad = cot_all[...] * sig * (1.0 + agg * (1.0 - sig))
    g_hi, g_lo = split(grad)
    q_send[...] = mm3(w_st[...], g_hi, g_lo, NN)

    def rows_of(ref, p):
        return ref.at[pl.ds(pl.multiple_of(fl * p, 8), fl), :]

    def q_copy(k):
        return remote(rows_of(q_send, feat_peer(k)), q_all.at[me], s_q, k - 1, f_dev(k))

    def q_recv(k):
        return remote(rows_of(q_send, me), q_all.at[feat_from(k)], s_q, k - 1, f_dev(k))

    loop(0, nf - 1, lambda i: q_copy(feat_order(i)).start())
    q_all[me] = q_send[pl.ds(pl.multiple_of(fl * me, 8), fl), :]

    g_st = jnp.concatenate([g_hi, g_lo], axis=0)
    terms = mm3(g_st, y_hi, y_lo, NT)
    for p in range(nf):
        wg_src[p % 2, p // 2] = terms[fl * p : fl * p + fl]
    pair = remote(wg_src.at[1 - my_core], wg_pair, s_wp, 0, to(dom, me + 1 - 2 * my_core))
    pair.start()

    def wf_copy(k):
        y = (my_y + k) % ny
        return remote(wg_half.at[y], wg_recv.at[k - 1], s_wf, k - 1, to(dom, y * 2 + my_core))

    def act_at(p):
        return act.at[:, pl.ds(pl.multiple_of(vw * p, 128), vw)]

    def act_copy(k):
        return remote(rows_of(act_send, feat_peer(k)), act_at(me), s_act, k - 1, f_dev(k))

    def act_recv(k):
        return remote(rows_of(act_send, me), act_at(feat_from(k)), s_act, k - 1, f_dev(k))

    loop(0, nf - 1, lambda i: act_copy(feat_order(i)).start())
    act_own = pltpu.make_async_copy(rows_of(act_send, me), act_at(me), s_misc.at[3])
    act_own.start()

    def hub_back(p):
        left = stacked(q_all[p])
        return mm3(left, adj_hi[p], adj_lo[p], NT)

    hub_acc[...] = hub_back(me)

    def hub_step(k):
        q_recv(k).wait_recv()
        hub_acc[...] += hub_back(feat_from(k))

    loop(1, nf, hub_step)
    hub_start(1)
    pair.wait_recv()
    wg_half[...] = wg_src[my_core] + wg_pair[...]
    for k in [2, 1, 3] if ny > 2 else []:
        wf_copy(k).start()

    def slot_terms(p):
        for j in range(pb):
            b = p * pb + j
            left = stacked(q_all[p, :, 128 * j : 128 * j + 128])
            out = mm3(left, cat_hi[b], cat_lo[b], NN)
            for k in range(slots):
                contrib[b * slots + k] = out[:, 128 * k : 128 * k + 128]

    loop(0, nf, slot_terms)

    def run_step(j, total):
        total = total * order[1, j].astype(F32) + contrib[order[0, j]]
        runs[j] = total
        return total

    lax.fori_loop(0, nb * slots, run_step, jnp.zeros((fl, 128), F32))

    def summed(block):
        return runs[order[2, block]] * order[3, block].astype(F32)

    def back_send(b):
        b_send[0, b] = summed(b)
        b_send[1, b] = summed(2 * nb + b)

    loop(0, nb, back_send)

    def back_copy(side, h):
        at = pl.ds(half * h, half)
        device = (to(prv, me), to(nxt, me))[side]
        return remote(b_send.at[side, at], b_recv.at[side, at], s_back.at[h], side, device)

    hub_z(1)
    both_sides(back_copy, 0)
    hub_zg(1)
    both_sides(back_copy, 1)

    term = wg_half[my_y]
    for k in range(1, ny):
        wf_copy(k).wait_recv()
        term += wg_recv[k - 1]
    part = full // nx
    for q in range(nx):
        wg_xsrc[q] = term[:, part * q : part * q + part]

    def wx_copy(k):
        return remote(wg_xsrc.at[x_peer(k)], wg_rx.at[k - 1], s_wx, k - 1, x_dev(k))

    for k in range(1, nx):
        wx_copy(k).start()

    hub_xg(1, 0)

    for k in range(1, nx):
        wx_copy(k).wait_recv()
    term = wg_xsrc[my_x]
    for k in range(1, nx):
        term += wg_rx[k - 1]
    term = term.T
    lanes = wg_zsrc.shape[2]
    if lanes > fl:
        term = jnp.concatenate([term, jnp.zeros((part, lanes - fl), F32)], axis=1)
    wg_zsrc[...] = term.reshape(wg_zsrc.shape)

    def wz_copy(k):
        return remote(wg_zsrc.at[z_peer(k)], wg_rz.at[k - 1], s_wz, k - 1, z_dev(k))

    loop(1, nz, lambda k: wz_copy(k).start())
    hub_xg(1, 1)

    hub_end(1)
    for h in range(2):
        back_copy(0, h).wait_recv()
        back_copy(1, h).wait_recv()

    def out_copy(p):
        return pltpu.make_async_copy(
            fg_out.at[p], fg.at[:, pl.ds(pl.multiple_of(vw * p, 128), vw)], s_out.at[p]
        )

    def finish(p):
        both = mm(hub_in[...], pick[p], NT)
        placed = both[:fl] + both[fl:]
        for j in range(pb):
            b = p * pb + j
            own = summed(nb + b)
            total = placed[:, 128 * j : 128 * j + 128] + own + b_recv[0, b] + b_recv[1, b]
            fg_out[p, :, 128 * j : 128 * j + 128] = total
        out_copy(p).start()

    loop(0, nf, finish)

    loop(1, nz, lambda k: wz_copy(k).wait_recv())
    term = wg_zsrc[my_z]
    for k in range(1, nz):
        term += wg_rz[k - 1]
    wg[...] = term[:, :fl] * (1.0 / math.sqrt(vl * nd))

    act_own.wait()
    loop(1, nf, lambda k: act_recv(k).wait_recv())
    pair.wait_send()
    for h in range(2):
        for side in range(2):
            ext_copy(side, h).wait_send()
            back_copy(side, h).wait_send()
    for k in range(1, ny):
        wf_copy(k).wait_send()

    def feat_sent(k):
        cot_copy(k).wait_send()
        y_copy(k).wait_send()
        q_copy(k).wait_send()
        act_copy(k).wait_send()

    loop(1, nf, feat_sent)
    for k in range(1, nx):
        for s in range(2):
            for h in range(2):
                x_rs_copy(s, k, h).wait_send()
                x_ag_copy(s, k, h).wait_send()
        wx_copy(k).wait_send()

    def z_sent(k):
        for s in range(2):
            z_rs_copy(s, k).wait_send()
            z_ag_copy(s, k).wait_send()
        wz_copy(k).wait_send()

    loop(1, nz, z_sent)
    loop(0, nf, lambda p: out_copy(p).wait())


def hand_over_kernel(count, *refs):
    ins, outs = refs[:count], refs[count : 2 * count]
    held, sems = refs[2 * count : 3 * count], refs[-1]
    reads = [pltpu.make_async_copy(ins[i], held[i], sems.at[0, i]) for i in range(count)]
    writes = [pltpu.make_async_copy(held[i], outs[i], sems.at[1, i]) for i in range(count)]
    for read in reads:
        read.start()
    for read, write in zip(reads, writes):
        read.wait()
        write.start()
    for write in writes:
        write.wait()


def hand_over(arrays):
    hbm = pl.BlockSpec(memory_space=pl.ANY)
    count = len(arrays)
    return pl.pallas_call(
        functools.partial(hand_over_kernel, count),
        out_shape=tuple(jax.ShapeDtypeStruct(a.shape, a.dtype) for a in arrays),
        in_specs=[hbm] * count,
        out_specs=(hbm,) * count,
        scratch_shapes=[pltpu.VMEM(a.shape, a.dtype) for a in arrays]
        + [pltpu.SemaphoreType.DMA((2, count))],
        compiler_params=pltpu.CompilerParams(vmem_limit_bytes=60 * 1024 * 1024),
    )(*arrays)


def local(nd, nf, nx, node_feats, weight, tiles, block_cols, block_count, hub_ids, hub_adj, cotangent):
    nz = nd // nx
    fl, vl = node_feats.shape
    full = weight.shape[0]
    nb, slots = block_cols.shape
    nh = hub_adj.shape[0]
    vw = vl // nf
    entries = nb * slots
    ny = nf // 2
    far = 7 if nz == 16 else 1
    z_near = (nz - far) // 2
    groups = (far, z_near + 1, z_near)
    lanes = max(fl, 128)
    vm = pltpu.VMEM
    dma = pltpu.SemaphoreType.DMA
    hub_tile = (8, 128)
    scratch = [
        vm((3 * nb, fl, 128), F32),
        vm((nf, nh, vw), F32), vm((nf, nh, vw), BF16), vm((nf, nh, vw), BF16),
        vm((nb, slots, 128, 128), F32),
        vm((nb, 128, slots * 128), BF16), vm((nb, 128, slots * 128), BF16),
        vm((nf, vw, nh), BF16),
        vm((full, full), F32), vm((2 * full, full), BF16), vm((2 * full, full), BF16),
        vm((nf, fl, vw), F32), vm((full, vw), F32), vm((full, vw), F32), vm((full, vw), F32),
        vm((full, vw), F32), vm((nf, fl, vw), F32),
        vm((fl, nh), F32), vm((2 * fl, nh), BF16),
        vm((entries, fl, 128), F32), vm((entries, fl, 128), F32),
        vm((2, nb, fl, 128), F32), vm((2, nb, fl, 128), F32), vm((nf, fl, vw), F32),
        vm((8, 128), jnp.int32), pltpu.SMEM((8, 128), jnp.int32),
        vm((2, nx, nz) + hub_tile, F32), vm((2, nx - 1, nz) + hub_tile, F32),
        vm((2, nz) + hub_tile, F32), vm((2, nz - 1) + hub_tile, F32),
        vm((2, nz) + hub_tile, F32), vm((2, nx, nz) + hub_tile, F32),
        vm((2, ny, fl, full), F32), vm((ny, fl, full), F32), vm((ny, fl, full), F32),
        vm((max(ny - 1, 1), fl, full), F32),
        vm((nx, fl, full // nx), F32), vm((nx - 1, fl, full // nx), F32),
        vm((nz, full // nx // nz, lanes), F32), vm((nz - 1, full // nx // nz, lanes), F32),
        dma((nb,)), dma((4,)), dma((nf,)), dma, dma((nf,)),
        dma((2, 2, 2)), dma((2, nf - 1)), dma((2, nf - 1)), dma((2, nf - 1)), dma((2, nf - 1)),
        dma((2, 2, 2)),
        dma((2, 2, 2, nx - 1)), dma((2, 2, nz - 1)), dma((2, 2, nz - 1)), dma((2, 2, 2, nx - 1)),
        dma((2, 1)), dma((2, max(ny - 1, 1))), dma((2, nx - 1)), dma((2, nz - 1)),
    ]
    hbm = pl.BlockSpec(memory_space=pl.ANY)
    vmem = pl.BlockSpec(memory_space=pltpu.VMEM)
    smem = pl.BlockSpec(memory_space=pltpu.SMEM)
    results = pl.pallas_call(
        functools.partial(kernel, (nx, nz, nf, nb, slots), groups),
        out_shape=(
            jax.ShapeDtypeStruct((fl, vl), F32),
            jax.ShapeDtypeStruct((fl, vl), F32),
            jax.ShapeDtypeStruct((full // nd, fl), F32),
        ),
        in_specs=[hbm] * 5 + [vmem] * 2 + [smem] * 2,
        out_specs=(hbm, hbm, vmem),
        scratch_shapes=scratch,
        compiler_params=pltpu.CompilerParams(
            collective_id=0, has_side_effects=True, vmem_limit_bytes=60 * 1024 * 1024
        ),
    )(
        node_feats, weight, tiles, hub_adj, cotangent, hub_ids.reshape(nh // 128, 128),
        block_cols, block_cols, block_count,
    )
    return hand_over(results)


def solution(mesh):
    nd, nf = mesh.shape["dom"], mesh.shape["feat"]
    nx = 4 if nd == 64 else 2
    return jax.shard_map(
        functools.partial(local, nd, nf, nx),
        mesh=mesh,
        in_specs=(
            P("feat", "dom"),
            P(),
            P("dom", None, None, None),
            P("dom", None),
            P("dom"),
            P(),
            P(None, "dom"),
            P("feat", "dom"),
        ),
        out_specs=(P("feat", "dom"), P("feat", "dom"), P("dom", "feat")),
        check_vma=False,
    )
```

```python
import functools
import math

import jax
import jax.numpy as jnp
from jax import lax
from jax.experimental import pallas as pl
from jax.experimental.pallas import tpu as pltpu
from jax.sharding import PartitionSpec as P

MESH = pl.DeviceIdType.MESH
F32 = jnp.float32
BF16 = jnp.bfloat16
NN = (((1,), (0,)), ((), ()))
NT = (((1,), (1,)), ((), ()))


def split(value):
    high = value.astype(BF16)
    low = (value - high.astype(F32)).astype(BF16)
    return high, low


def mm(a, b, dims):
    return lax.dot_general(a, b, dims, preferred_element_type=F32)


def stacked(value):
    high, low = split(value)
    return jnp.concatenate([high, low], axis=0)


def mm3(left, right_high, right_low, dims):
    rows = left.shape[0] // 2
    both = mm(left, right_high, dims)
    return both[:rows] + both[rows:] + mm(left[:rows], right_low, dims)


def kernel(
    sizes,
    x, w, tiles, hub_adj, cot, ids, cols_v, cols, count,
    act, fg, wg,
    ext, adj_f32, adj_hi, adj_lo, tiles_f32, cat_hi, cat_lo, pick,
    w_f32, w_st, wt_st, y_send, y_all, cot_all, act_send, q_send, q_all,
    hub_acc, hub_in, contrib, runs, b_send, b_recv, fg_out, order_v, order,
    h_src, h_rx, h_zsrc, h_rz, h_zg, h_xg,
    wg_src, wg_pair, wg_half, wg_recv, wg_xsrc, wg_rx, wg_zsrc, wg_rz,
    s_x, s_misc, s_adj, s_cot_own, s_out,
    s_nbr, s_cot, s_y, s_q, s_act, s_back, s_hx, s_hz, s_hzg, s_hxg, s_wp, s_wf, s_wx, s_wz,
):
    nx, nz, nf, nb, slots = sizes
    ny = nf // 2
    nd = nx * nz
    fl, vl = x.shape
    full = w.shape[0]
    nh = hub_adj.shape[0]
    pb = nb // nf
    vw = pb * 128
    row_tiles = fl // 8
    per_q = nh // 128 // nx
    dom = lax.axis_index("dom")
    me = lax.axis_index("feat")
    my_x, my_z = dom // nz, dom % nz
    my_y, my_core = me // 2, me % 2
    nxt, prv = (dom + 1) % nd, (dom + nd - 1) % nd

    def feat_peer(k):
        return (me + k) % nf

    def feat_from(k):
        return (me + nf - k) % nf

    def x_peer(k):
        return (my_x + k) % nx

    def z_peer(k):
        return (my_z + k) % nz

    def z_step(o):
        return (nz // 2 + (1 - 2 * (o % 2)) * ((o + 1) // 2) + nz) % nz

    def z_back(o):
        return o + (2 * (o % 2) - 1) * ((o + nz - 1) // nz)

    def to(domain, feature):
        return {"dom": domain, "feat": feature}

    def x_dev(k):
        return to(x_peer(k) * nz + my_z, me)

    def z_dev(k):
        return to(my_x * nz + z_peer(k), me)

    def f_dev(k):
        return to(dom, feat_peer(k))

    def remote(src, dst, sems, at, device):
        return pltpu.make_async_remote_copy(
            src_ref=src, dst_ref=dst, send_sem=sems.at[0, at], recv_sem=sems.at[1, at],
            device_id=device, device_id_type=MESH,
        )

    def loop(lower, upper, body):
        def step(i, carry):
            body(i)
            return carry

        lax.fori_loop(lower, upper, step, 0)

    barrier = pltpu.get_barrier_semaphore()

    def greet(device):
        pl.semaphore_signal(barrier, inc=1, device_id=device, device_id_type=MESH)

    loop(0, nz - 1, lambda o: greet(z_dev(z_step(o))))
    for k in range(1, nx):
        greet(x_dev(k))
    greet(to(nxt, me))
    greet(to(prv, me))
    loop(1, nf, lambda k: greet(f_dev(k)))
    x_loads = [
        pltpu.make_async_copy(x.at[:, pl.ds(128 * b, 128)], ext.at[nb + b], s_x.at[b])
        for b in range(nb)
    ]
    for copy in x_loads:
        copy.start()
    tiles_load = pltpu.make_async_copy(tiles, tiles_f32, s_misc.at[0])
    w_load = pltpu.make_async_copy(w, w_f32, s_misc.at[1])
    adj_loads = [
        pltpu.make_async_copy(hub_adj.at[:, pl.ds(vw * p, vw)], adj_f32.at[p], s_adj.at[p])
        for p in range(nf)
    ]
    cot_own = pltpu.make_async_copy(
        cot.at[:, pl.ds(pl.multiple_of(vw * me, 128), vw)],
        cot_all.at[pl.ds(pl.multiple_of(fl * me, 8), fl), :], s_cot_own,
    )
    tiles_load.start()
    w_load.start()
    cot_own.start()
    for copy in adj_loads:
        copy.start()

    for copy in x_loads:
        copy.wait()

    half = nb // 2

    def ext_copy(side, h):
        at, device = ((0, to(nxt, me)), (2 * nb, to(prv, me)))[side]
        return remote(
            ext.at[pl.ds(nb + half * h, half)], ext.at[pl.ds(at + half * h, half)],
            s_nbr.at[h], side, device,
        )

    def both_sides(copies, h):
        copies(0, h).start()
        copies(1, h).start()

    def cot_copy(k):
        p = feat_peer(k)
        return remote(
            cot.at[:, pl.ds(pl.multiple_of(vw * p, 128), vw)],
            cot_all.at[pl.ds(pl.multiple_of(fl * me, 8), fl), :], s_cot, k - 1, f_dev(k),
        )

    local_id = ids[...] - dom * vl
    hub_acc[...] = jnp.zeros_like(hub_acc)

    def own_hubs(p):
        row = lax.broadcasted_iota(jnp.int32, (vw, 128), 0) + p * vw
        chunk = jnp.concatenate(
            [
                jnp.where(row == local_id[g : g + 1], 1.0, 0.0).astype(BF16)
                for g in range(nh // 128)
            ],
            axis=1,
        )
        pick[p] = chunk
        left = stacked(jnp.concatenate([ext[nb + pb * p + j] for j in range(pb)], axis=1))
        both = mm(left, chunk, NN)
        hub_acc[...] += both[:fl] + both[fl:]

    loop(0, nf, own_hubs)

    pl.semaphore_wait(barrier, 2 + (nx - 1) + (nz - 1) + (nf - 1))

    cuts = (0, 3, 9, nz) if nz == 16 else (0, 1, nz)
    pieces = [(cuts[i], cuts[i + 1]) for i in range(len(cuts) - 1)]
    own_at = nz - 1

    def piece(h):
        lower, upper = pieces[h]
        return pl.ds(lower, upper - lower)

    def z_loop(h, body):
        lower, upper = pieces[h]
        loop(lower, min(upper, nz - 1), body)

    def x_rs_copy(s, k, h):
        at = piece(h)
        return remote(
            h_src.at[s, x_peer(k), at], h_rx.at[s, k - 1, at], s_hx.at[s, h], k - 1, x_dev(k)
        )

    def z_rs_copy(s, o):
        return remote(h_zsrc.at[s, o], h_rz.at[s, o], s_hz.at[s], o, z_dev(z_step(o)))

    def z_ag_copy(s, o):
        dst = h_zg.at[s, z_back(o)]
        return remote(h_zg.at[s, own_at], dst, s_hzg.at[s], o, z_dev(z_step(o)))

    def x_ag_copy(s, k, h):
        at = piece(h)
        return remote(h_zg.at[s, at], h_xg.at[s, k, at], s_hxg.at[s, h], k - 1, x_dev(k))

    x_order = [2, 1, 3][:nx] if nx > 2 else [1]

    def z_place(i):
        step = (i + nz - my_z) % nz
        down = 2 * (nz // 2 - step) - 1
        up = 2 * (step - nz // 2)
        return jnp.where(step < nz // 2, down, up)

    def hub_start(s):
        for q in range(nx):
            for i in range(nz):
                r, c = i // per_q, q * per_q + i % per_q
                h_src[s, q, z_place(i)] = hub_acc[8 * r : 8 * r + 8, 128 * c : 128 * c + 128]
        for h in range(len(pieces)):
            for k in x_order:
                x_rs_copy(s, k, h).start()

    def hub_z(s):
        for h in range(len(pieces)):
            for k in x_order:
                x_rs_copy(s, k, h).wait_recv()
            at = piece(h)
            total = h_src[s, my_x, at]
            for k in range(1, nx):
                total += h_rx[s, k - 1, at]
            h_zsrc[s, at] = total
            z_loop(h, lambda o: z_rs_copy(s, o).start())

    def hub_zg(s):
        loop(0, nz - 1, lambda o: z_rs_copy(s, o).wait_recv())
        total = h_zsrc[s, own_at]
        for o in range(nz - 1):
            total += h_rz[s, o]
        h_zg[s, own_at] = total
        loop(0, nz - 1, lambda o: z_ag_copy(s, o).start())

    def hub_xg(s, h):
        z_loop(h, lambda o: z_ag_copy(s, o).wait_recv())
        for k in x_order:
            x_ag_copy(s, k, h).start()
        at = piece(h)
        h_xg[s, 0, at] = h_zg[s, at]

    def hub_end(s):
        for h in reversed(range(len(pieces))):
            for k in x_order:
                x_ag_copy(s, k, h).wait_recv()
        for q in range(nx):
            for i in range(nz):
                r, c = i // per_q, q * per_q + i % per_q
                tile = h_xg[s, (my_x + nx - q) % nx, z_place(i)]
                hub_acc[8 * r : 8 * r + 8, 128 * c : 128 * c + 128] = tile
        hub_in[...] = stacked(hub_acc[...])

    hub_start(0)
    tiles_load.wait()

    def split_tiles(b):
        both = [split(tiles_f32[b, k]) for k in range(slots)]
        cat_hi[b] = jnp.concatenate([one[0] for one in both], axis=1)
        cat_lo[b] = jnp.concatenate([one[1] for one in both], axis=1)

    loop(0, nb, split_tiles)
    hub_z(0)
    both_sides(ext_copy, 0)
    loop(1, nf, lambda k: cot_copy(k).start())

    entries = nb * slots
    none = 3 * nb
    row = lax.broadcasted_iota(jnp.int32, (slots, nb), 0)
    lane = lax.broadcasted_iota(jnp.int32, (slots, nb), 1)
    place = lane * slots + row
    counts = jnp.zeros((slots, nb), jnp.int32)
    for b in range(nb):
        counts = jnp.where(lane == b, count[b], counts)
    target = jnp.where(row < counts, cols_v[...], none)
    along = lax.broadcasted_iota(jnp.int32, (1, 128), 1)

    def one(flag):
        return jnp.where(flag, 1, 0)

    def rank_step(e, carry):
        rank, again, upto, found = carry
        b, k = e // slots, e % slots
        goal = jnp.where(k < count[b], cols[k, b], none)
        tie = one(target == goal) * one(place > e)
        return (
            rank + one(target > goal) + tie, jnp.maximum(again, tie),
            upto + one(along >= goal), jnp.maximum(found, one(along == goal)),
        )

    zero, zeros = jnp.zeros((slots, nb), jnp.int32), jnp.zeros((1, 128), jnp.int32)
    rank, again, upto, found = lax.fori_loop(0, entries, rank_step, (zero, zero, zeros, zeros))
    which, same = zeros, zeros
    for e in range(entries):
        b, k = e // slots, e % slots
        here = rank[k : k + 1, b : b + 1] == along
        which = jnp.where(here, e, which)
        same = jnp.where(here, again[k : k + 1, b : b + 1], same)
    order_v[0:1] = which
    order_v[1:2] = same
    order_v[2:3] = jnp.maximum(upto - 1, 0)
    order_v[3:4] = found
    order_copy = pltpu.make_async_copy(order_v, order, s_misc.at[2])
    order_copy.start()

    w_load.wait()
    w_st[...] = stacked(w_f32[...])
    wt_st[...] = stacked(w_f32[...].T)

    def split_adj(p):
        high, low = split(adj_f32[p])
        adj_hi[p] = high
        adj_lo[p] = low

    for copy in adj_loads:
        copy.wait()
    loop(0, nf // 2, split_adj)
    hub_zg(0)
    both_sides(ext_copy, 1)
    loop(nf // 2, nf, split_adj)
    order_copy.wait()
    for h in reversed(range(len(pieces))):
        hub_xg(0, h)

    for h in range(2):
        ext_copy(0, h).wait_recv()
        ext_copy(1, h).wait_recv()

    def tile_part(p):
        for j in range(pb):
            b = p * pb + j
            left = jnp.concatenate(
                [ext[cols[k, b]] * jnp.where(k < count[b], 1.0, 0.0) for k in range(slots)],
                axis=1,
            )
            y_send[p, :, 128 * j : 128 * j + 128] = mm3(stacked(left), cat_hi[b], cat_lo[b], NT)

    loop(0, nf, tile_part)
    hub_end(0)

    def y_copy(k):
        return remote(
            y_send.at[feat_peer(k)], y_all.at[pl.ds(pl.multiple_of(fl * me, 8), fl), :],
            s_y, k - 1, f_dev(k),
        )

    def y_recv(k):
        at = y_all.at[pl.ds(pl.multiple_of(fl * feat_from(k), 8), fl), :]
        return remote(y_send.at[0], at, s_y, k - 1, f_dev(k))

    def hub_to_y(p):
        return y_send[p] + mm3(hub_in[...], adj_hi[p], adj_lo[p], NN)

    def feat_order(i):
        return nf // 2 if nf < 4 else (nf // 2 + (1 - 2 * (i % 2)) * ((i + 1) // 2)) % nf

    def hub_part(i):
        k = feat_order(i)
        p = feat_peer(k)
        y_send[p] = hub_to_y(p)
        y_copy(k).start()

    loop(0, nf - 1, hub_part)
    y_all[pl.ds(pl.multiple_of(fl * me, 8), fl), :] = hub_to_y(me)

    loop(1, nf, lambda k: y_recv(k).wait_recv())
    y_hi, y_lo = split(y_all[...])
    agg = mm3(wt_st[...], y_hi, y_lo, NN)
    sig = 1.0 / (1.0 + jnp.exp(-agg))
    act_send[...] = agg * sig
    cot_own.wait()

    def cot_recv(k):
        at = cot_all.at[pl.ds(pl.multiple_of(fl * feat_from(k), 8), fl), :]
        return remote(cot.at[:, pl.ds(0, vw)], at, s_cot, k - 1, f_dev(k))

    loop(1, nf, lambda k: cot_recv(k).wait_recv())
    grad = cot_all[...] * sig * (1.0 + agg * (1.0 - sig))
    g_hi, g_lo = split(grad)
    q_send[...] = mm3(w_st[...], g_hi, g_lo, NN)

    def rows_of(ref, p):
        return ref.at[pl.ds(pl.multiple_of(fl * p, 8), fl), :]

    def q_copy(k):
        return remote(rows_of(q_send, feat_peer(k)), q_all.at[me], s_q, k - 1, f_dev(k))

    def q_recv(k):
        return remote(rows_of(q_send, me), q_all.at[feat_from(k)], s_q, k - 1, f_dev(k))

    loop(0, nf - 1, lambda i: q_copy(feat_order(i)).start())
    q_all[me] = q_send[pl.ds(pl.multiple_of(fl * me, 8), fl), :]

    g_st = jnp.concatenate([g_hi, g_lo], axis=0)
    terms = mm3(g_st, y_hi, y_lo, NT)
    for p in range(nf):
        wg_src[p % 2, p // 2] = terms[fl * p : fl * p + fl]
    pair = remote(wg_src.at[1 - my_core], wg_pair, s_wp, 0, to(dom, me + 1 - 2 * my_core))
    pair.start()

    def wf_copy(k):
        y = (my_y + k) % ny
        return remote(wg_half.at[y], wg_recv.at[k - 1], s_wf, k - 1, to(dom, y * 2 + my_core))

    def act_at(p):
        return act.at[:, pl.ds(pl.multiple_of(vw * p, 128), vw)]

    def act_copy(k):
        return remote(rows_of(act_send, feat_peer(k)), act_at(me), s_act, k - 1, f_dev(k))

    def act_recv(k):
        return remote(rows_of(act_send, me), act_at(feat_from(k)), s_act, k - 1, f_dev(k))

    act_own = pltpu.make_async_copy(rows_of(act_send, me), act_at(me), s_misc.at[3])
    act_own.start()

    def hub_back(p):
        left = stacked(q_all[p])
        return mm3(left, adj_hi[p], adj_lo[p], NT)

    hub_acc[...] = hub_back(me)

    def hub_step(k):
        q_recv(k).wait_recv()
        hub_acc[...] += hub_back(feat_from(k))

    loop(1, nf, hub_step)
    hub_start(1)
    pair.wait_recv()
    wg_half[...] = wg_src[my_core] + wg_pair[...]
    for k in [2, 1, 3] if ny > 2 else []:
        wf_copy(k).start()

    def slot_terms(p):
        for j in range(pb):
            b = p * pb + j
            left = stacked(q_all[p, :, 128 * j : 128 * j + 128])
            out = mm3(left, cat_hi[b], cat_lo[b], NN)
            for k in range(slots):
                contrib[b * slots + k] = out[:, 128 * k : 128 * k + 128]

    loop(0, nf, slot_terms)

    def run_step(j, total):
        total = total * order[1, j].astype(F32) + contrib[order[0, j]]
        runs[j] = total
        return total

    lax.fori_loop(0, nb * slots, run_step, jnp.zeros((fl, 128), F32))

    def summed(block):
        return runs[order[2, block]] * order[3, block].astype(F32)

    def back_send(b):
        b_send[0, b] = summed(b)
        b_send[1, b] = summed(2 * nb + b)

    loop(0, nb, back_send)

    def back_copy(side, h):
        at = pl.ds(half * h, half)
        device = (to(prv, me), to(nxt, me))[side]
        return remote(b_send.at[side, at], b_recv.at[side, at], s_back.at[h], side, device)

    hub_z(1)
    both_sides(back_copy, 0)

    term = wg_half[my_y]
    for k in range(1, ny):
        wf_copy(k).wait_recv()
        term += wg_recv[k - 1]
    part = full // nx
    for q in range(nx):
        wg_xsrc[q] = term[:, part * q : part * q + part]

    def wx_copy(k):
        return remote(wg_xsrc.at[x_peer(k)], wg_rx.at[k - 1], s_wx, k - 1, x_dev(k))

    for k in range(1, nx):
        wx_copy(k).start()

    hub_zg(1)
    both_sides(back_copy, 1)
    loop(0, nf - 1, lambda i: act_copy(feat_order(i)).start())

    for k in range(1, nx):
        wx_copy(k).wait_recv()
    term = wg_xsrc[my_x]
    for k in range(1, nx):
        term += wg_rx[k - 1]
    term = term.T
    lanes = wg_zsrc.shape[2]
    if lanes > fl:
        term = jnp.concatenate([term, jnp.zeros((part, lanes - fl), F32)], axis=1)
    wg_zsrc[...] = term.reshape(wg_zsrc.shape)

    def wz_copy(k):
        return remote(wg_zsrc.at[z_peer(k)], wg_rz.at[k - 1], s_wz, k - 1, z_dev(k))

    loop(1, nz, lambda k: wz_copy(k).start())

    for h in reversed(range(len(pieces))):
        hub_xg(1, h)


    hub_end(1)
    for h in range(2):
        back_copy(0, h).wait_recv()
        back_copy(1, h).wait_recv()

    def out_copy(p):
        return pltpu.make_async_copy(
            fg_out.at[p], fg.at[:, pl.ds(pl.multiple_of(vw * p, 128), vw)], s_out.at[p]
        )

    def finish(p):
        both = mm(hub_in[...], pick[p], NT)
        placed = both[:fl] + both[fl:]
        for j in range(pb):
            b = p * pb + j
            own = summed(nb + b)
            total = placed[:, 128 * j : 128 * j + 128] + own + b_recv[0, b] + b_recv[1, b]
            fg_out[p, :, 128 * j : 128 * j + 128] = total
        out_copy(p).start()

    loop(0, nf, finish)

    loop(1, nz, lambda k: wz_copy(k).wait_recv())
    term = wg_zsrc[my_z]
    for k in range(1, nz):
        term += wg_rz[k - 1]
    wg[...] = term[:, :fl] * (1.0 / math.sqrt(vl * nd))

    act_own.wait()
    loop(1, nf, lambda k: act_recv(k).wait_recv())
    pair.wait_send()
    for h in range(2):
        for side in range(2):
            ext_copy(side, h).wait_send()
            back_copy(side, h).wait_send()
    for k in range(1, ny):
        wf_copy(k).wait_send()

    def feat_sent(k):
        cot_copy(k).wait_send()
        y_copy(k).wait_send()
        q_copy(k).wait_send()
        act_copy(k).wait_send()

    loop(1, nf, feat_sent)
    for k in range(1, nx):
        for s in range(2):
            for h in range(len(pieces)):
                x_rs_copy(s, k, h).wait_send()
                x_ag_copy(s, k, h).wait_send()
        wx_copy(k).wait_send()

    def z_sent(o):
        for s in range(2):
            z_rs_copy(s, o).wait_send()
            z_ag_copy(s, o).wait_send()
        wz_copy(o + 1).wait_send()

    loop(0, nz - 1, z_sent)
    loop(0, nf, lambda p: out_copy(p).wait())


def hand_over_kernel(count, *refs):
    ins, outs = refs[:count], refs[count : 2 * count]
    held, sems = refs[2 * count : 3 * count], refs[-1]
    reads = [pltpu.make_async_copy(ins[i], held[i], sems.at[0, i]) for i in range(count)]
    writes = [pltpu.make_async_copy(held[i], outs[i], sems.at[1, i]) for i in range(count)]
    for read in reads:
        read.start()
    for read, write in zip(reads, writes):
        read.wait()
        write.start()
    for write in writes:
        write.wait()


def hand_over(arrays):
    hbm = pl.BlockSpec(memory_space=pl.ANY)
    count = len(arrays)
    return pl.pallas_call(
        functools.partial(hand_over_kernel, count),
        out_shape=tuple(jax.ShapeDtypeStruct(a.shape, a.dtype) for a in arrays),
        in_specs=[hbm] * count,
        out_specs=(hbm,) * count,
        scratch_shapes=[pltpu.VMEM(a.shape, a.dtype) for a in arrays]
        + [pltpu.SemaphoreType.DMA((2, count))],
        compiler_params=pltpu.CompilerParams(vmem_limit_bytes=60 * 1024 * 1024),
    )(*arrays)


def local(nd, nf, nx, node_feats, weight, tiles, block_cols, block_count, hub_ids, hub_adj, cotangent):
    nz = nd // nx
    fl, vl = node_feats.shape
    full = weight.shape[0]
    nb, slots = block_cols.shape
    nh = hub_adj.shape[0]
    vw = vl // nf
    entries = nb * slots
    ny = nf // 2
    lanes = max(fl, 128)
    vm = pltpu.VMEM
    dma = pltpu.SemaphoreType.DMA
    hub_tile = (8, 128)
    scratch = [
        vm((3 * nb, fl, 128), F32),
        vm((nf, nh, vw), F32), vm((nf, nh, vw), BF16), vm((nf, nh, vw), BF16),
        vm((nb, slots, 128, 128), F32),
        vm((nb, 128, slots * 128), BF16), vm((nb, 128, slots * 128), BF16),
        vm((nf, vw, nh), BF16),
        vm((full, full), F32), vm((2 * full, full), BF16), vm((2 * full, full), BF16),
        vm((nf, fl, vw), F32), vm((full, vw), F32), vm((full, vw), F32), vm((full, vw), F32),
        vm((full, vw), F32), vm((nf, fl, vw), F32),
        vm((fl, nh), F32), vm((2 * fl, nh), BF16),
        vm((entries, fl, 128), F32), vm((entries, fl, 128), F32),
        vm((2, nb, fl, 128), F32), vm((2, nb, fl, 128), F32), vm((nf, fl, vw), F32),
        vm((8, 128), jnp.int32), pltpu.SMEM((8, 128), jnp.int32),
        vm((2, nx, nz) + hub_tile, F32), vm((2, nx - 1, nz) + hub_tile, F32),
        vm((2, nz) + hub_tile, F32), vm((2, nz - 1) + hub_tile, F32),
        vm((2, nz) + hub_tile, F32), vm((2, nx, nz) + hub_tile, F32),
        vm((2, ny, fl, full), F32), vm((ny, fl, full), F32), vm((ny, fl, full), F32),
        vm((max(ny - 1, 1), fl, full), F32),
        vm((nx, fl, full // nx), F32), vm((nx - 1, fl, full // nx), F32),
        vm((nz, full // nx // nz, lanes), F32), vm((nz - 1, full // nx // nz, lanes), F32),
        dma((nb,)), dma((4,)), dma((nf,)), dma, dma((nf,)),
        dma((2, 2, 2)), dma((2, nf - 1)), dma((2, nf - 1)), dma((2, nf - 1)), dma((2, nf - 1)),
        dma((2, 2, 2)),
        dma((2, 3, 2, nx - 1)), dma((2, 2, nz - 1)), dma((2, 2, nz - 1)), dma((2, 3, 2, nx - 1)),
        dma((2, 1)), dma((2, max(ny - 1, 1))), dma((2, nx - 1)), dma((2, nz - 1)),
    ]
    hbm = pl.BlockSpec(memory_space=pl.ANY)
    vmem = pl.BlockSpec(memory_space=pltpu.VMEM)
    smem = pl.BlockSpec(memory_space=pltpu.SMEM)
    results = pl.pallas_call(
        functools.partial(kernel, (nx, nz, nf, nb, slots)),
        out_shape=(
            jax.ShapeDtypeStruct((fl, vl), F32),
            jax.ShapeDtypeStruct((fl, vl), F32),
            jax.ShapeDtypeStruct((full // nd, fl), F32),
        ),
        in_specs=[hbm] * 5 + [vmem] * 2 + [smem] * 2,
        out_specs=(hbm, hbm, vmem),
        scratch_shapes=scratch,
        compiler_params=pltpu.CompilerParams(
            collective_id=0, has_side_effects=True, vmem_limit_bytes=60 * 1024 * 1024
        ),
    )(
        node_feats, weight, tiles, hub_adj, cotangent, hub_ids.reshape(nh // 128, 128),
        block_cols.T, block_cols.T, block_count,
    )
    return hand_over(results)


def solution(mesh):
    nd, nf = mesh.shape["dom"], mesh.shape["feat"]
    nx = 4 if nd == 64 else 2
    return jax.shard_map(
        functools.partial(local, nd, nf, nx),
        mesh=mesh,
        in_specs=(
            P("feat", "dom"),
            P(),
            P("dom", None, None, None),
            P("dom", None),
            P("dom"),
            P(),
            P(None, "dom"),
            P("feat", "dom"),
        ),
        out_specs=(P("feat", "dom"), P("feat", "dom"), P("dom", "feat")),
        check_vma=False,
    )
```

```python
import functools
import math

import jax
import jax.numpy as jnp
from jax import lax
from jax.experimental import pallas as pl
from jax.experimental.pallas import tpu as pltpu
from jax.sharding import PartitionSpec as P

MESH = pl.DeviceIdType.MESH
F32 = jnp.float32
BF16 = jnp.bfloat16
NN = (((1,), (0,)), ((), ()))
NT = (((1,), (1,)), ((), ()))
THERE = ((), (0, 1), (2, 3))
BACK = ((), (0, 1), (2, 3))


def split(value):
    high = value.astype(BF16)
    low = (value - high.astype(F32)).astype(BF16)
    return high, low


def mm(a, b, dims):
    return lax.dot_general(a, b, dims, preferred_element_type=F32)


def stacked(value):
    high, low = split(value)
    return jnp.concatenate([high, low], axis=0)


def mm3(left, right_high, right_low, dims):
    rows = left.shape[0] // 2
    both = mm(left, right_high, dims)
    return both[:rows] + both[rows:] + mm(left[:rows], right_low, dims)


def kernel(
    sizes,
    x, w, tiles, hub_adj, cot, ids, cols_v, cols, count,
    act, fg, wg,
    ext, adj_f32, adj_hi, adj_lo, tiles_f32, cat_hi, cat_lo, pick,
    w_f32, w_st, wt_st, y_send, y_all, cot_all, act_send, q_send, q_all,
    hub_acc, hub_in, contrib, runs, b_send, b_recv, fg_out, order_v, order,
    h_src, h_rx, h_zsrc, h_rz, h_zg, h_xg,
    wg_src, wg_pair, wg_half, wg_recv, wg_xsrc, wg_rx, wg_zsrc, wg_rz,
    s_x, s_misc, s_adj, s_cot_own, s_out,
    s_nbr, s_cot, s_y, s_q, s_act, s_back, s_hx, s_hz, s_hzg, s_hxg, s_wp, s_wf, s_wx, s_wz,
):
    nx, nz, nf, nb, slots = sizes
    ny = nf // 2
    nd = nx * nz
    fl, vl = x.shape
    full = w.shape[0]
    nh = hub_adj.shape[0]
    pb = nb // nf
    vw = pb * 128
    row_tiles = fl // 8
    per_q = nh // 128 // nx
    dom = lax.axis_index("dom")
    me = lax.axis_index("feat")
    my_x, my_z = dom // nz, dom % nz
    my_y, my_core = me // 2, me % 2
    nxt, prv = (dom + 1) % nd, (dom + nd - 1) % nd

    def feat_peer(k):
        return (me + k) % nf

    def feat_from(k):
        return (me + nf - k) % nf

    def x_peer(k):
        return (my_x + k) % nx

    def z_peer(k):
        return (my_z + k) % nz

    def z_step(o):
        return (nz // 2 + (1 - 2 * (o % 2)) * ((o + 1) // 2) + nz) % nz

    def z_back(o):
        return o + (2 * (o % 2) - 1) * ((o + nz - 1) // nz)

    def to(domain, feature):
        return {"dom": domain, "feat": feature}

    def x_dev(k):
        return to(x_peer(k) * nz + my_z, me)

    def z_dev(k):
        return to(my_x * nz + z_peer(k), me)

    def f_dev(k):
        return to(dom, feat_peer(k))

    def remote(src, dst, sent, came, device):
        return pltpu.make_async_remote_copy(
            src_ref=src, dst_ref=dst, send_sem=sent, recv_sem=came,
            device_id=device, device_id_type=MESH,
        )

    def wait_for(ref, sem):
        pltpu.make_async_copy(ref, ref, sem).wait()

    def loop(lower, upper, body):
        def step(i, carry):
            body(i)
            return carry

        lax.fori_loop(lower, upper, step, 0)

    barrier = pltpu.get_barrier_semaphore()

    def greet(device):
        pl.semaphore_signal(barrier, inc=1, device_id=device, device_id_type=MESH)

    loop(0, nz - 1, lambda o: greet(z_dev(z_step(o))))
    for k in range(1, nx):
        greet(x_dev(k))
    greet(to(nxt, me))
    greet(to(prv, me))
    loop(1, nf, lambda k: greet(f_dev(k)))
    x_loads = [
        pltpu.make_async_copy(x.at[:, pl.ds(128 * b, 128)], ext.at[nb + b], s_x)
        for b in range(nb)
    ]
    for copy in x_loads:
        copy.start()
    tiles_load = pltpu.make_async_copy(tiles, tiles_f32, s_misc.at[0])
    w_load = pltpu.make_async_copy(w, w_f32, s_misc.at[1])
    adj_loads = [
        pltpu.make_async_copy(hub_adj.at[:, pl.ds(vw * p, vw)], adj_f32.at[p], s_adj)
        for p in range(nf)
    ]
    cot_own = pltpu.make_async_copy(
        cot.at[:, pl.ds(pl.multiple_of(vw * me, 128), vw)],
        cot_all.at[pl.ds(pl.multiple_of(fl * me, 8), fl), :], s_cot_own,
    )
    tiles_load.start()
    w_load.start()
    cot_own.start()
    for copy in adj_loads:
        copy.start()

    wait_for(ext.at[pl.ds(nb, nb)], s_x)

    quarter = nb // 4

    def ext_copy(side, h):
        at, device = ((0, to(nxt, me)), (2 * nb, to(prv, me)))[side]
        return remote(
            ext.at[pl.ds(nb + quarter * h, quarter)], ext.at[pl.ds(at + quarter * h, quarter)],
            s_nbr.at[0], s_nbr.at[1], device,
        )

    def both_sides(copies, which):
        for h in which:
            copies(0, h).start()
            copies(1, h).start()

    def cot_copy(k):
        p = feat_peer(k)
        return remote(
            cot.at[:, pl.ds(pl.multiple_of(vw * p, 128), vw)],
            cot_all.at[pl.ds(pl.multiple_of(fl * me, 8), fl), :], s_cot.at[0], s_cot.at[1],
            f_dev(k),
        )

    local_id = ids[...] - dom * vl
    hub_acc[...] = jnp.zeros_like(hub_acc)

    def own_hubs(p):
        row = lax.broadcasted_iota(jnp.int32, (vw, 128), 0) + p * vw
        chunk = jnp.concatenate(
            [
                jnp.where(row == local_id[g : g + 1], 1.0, 0.0).astype(BF16)
                for g in range(nh // 128)
            ],
            axis=1,
        )
        pick[p] = chunk
        left = stacked(jnp.concatenate([ext[nb + pb * p + j] for j in range(pb)], axis=1))
        both = mm(left, chunk, NN)
        hub_acc[...] += both[:fl] + both[fl:]

    loop(0, nf, own_hubs)

    pl.semaphore_wait(barrier, 2 + (nx - 1) + (nz - 1) + (nf - 1))

    cuts = (0, 3, 9, nz) if nz == 16 else (0, 1, nz)
    pieces = [(cuts[i], cuts[i + 1]) for i in range(len(cuts) - 1)]
    own_at = nz - 1

    def piece(h):
        lower, upper = pieces[h]
        return pl.ds(lower, upper - lower)

    def z_loop(h, body):
        lower, upper = pieces[h]
        loop(lower, min(upper, nz - 1), body)

    def x_rs_copy(s, k, h):
        at = piece(h)
        return remote(
            h_src.at[s, x_peer(k), at], h_rx.at[s, k - 1, at], s_hx.at[s, 3], s_hx.at[s, h],
            x_dev(k),
        )

    def z_rs_copy(s, o):
        sent, came = s_hz.at[s, 0], s_hz.at[s, 1]
        return remote(h_zsrc.at[s, o], h_rz.at[s, o], sent, came, z_dev(z_step(o)))

    def z_ag_copy(s, o, h):
        dst = h_zg.at[s, z_back(o)]
        return remote(h_zg.at[s, own_at], dst, s_hzg.at[s, 3], s_hzg.at[s, h], z_dev(z_step(o)))

    def x_ag_copy(s, k, h):
        at = piece(h)
        return remote(h_zg.at[s, at], h_xg.at[s, k, at], s_hxg.at[s, 0], s_hxg.at[s, 1], x_dev(k))

    x_order = [2, 1, 3][:nx] if nx > 2 else [1]

    def z_place(i):
        step = (i + nz - my_z) % nz
        down = 2 * (nz // 2 - step) - 1
        up = 2 * (step - nz // 2)
        return jnp.where(step < nz // 2, down, up)

    def hub_start(s):
        for q in range(nx):
            for i in range(nz):
                r, c = i // per_q, q * per_q + i % per_q
                h_src[s, q, z_place(i)] = hub_acc[8 * r : 8 * r + 8, 128 * c : 128 * c + 128]
        for h in range(len(pieces)):
            for k in x_order:
                x_rs_copy(s, k, h).start()

    def hub_z(s):
        for h in range(len(pieces)):
            at = piece(h)
            wait_for(h_rx.at[s, :, at], s_hx.at[s, h])
            total = h_src[s, my_x, at]
            for k in range(1, nx):
                total += h_rx[s, k - 1, at]
            h_zsrc[s, at] = total
            z_loop(h, lambda o: z_rs_copy(s, o).start())

    def hub_zg(s):
        wait_for(h_rz.at[s], s_hz.at[s, 1])
        total = h_zsrc[s, own_at]
        for o in range(nz - 1):
            total += h_rz[s, o]
        h_zg[s, own_at] = total
        for h in range(len(pieces)):
            z_loop(h, lambda o: z_ag_copy(s, o, h).start())

    def hub_xg(s, h):
        lower, upper = pieces[h]
        if min(upper, nz - 1) > lower:
            wait_for(h_zg.at[s, pl.ds(lower, min(upper, nz - 1) - lower)], s_hzg.at[s, h])
        for k in x_order:
            x_ag_copy(s, k, h).start()
        at = piece(h)
        h_xg[s, 0, at] = h_zg[s, at]

    def hub_end(s):
        wait_for(h_xg.at[s, pl.ds(1, nx - 1)], s_hxg.at[s, 1])
        for q in range(nx):
            for i in range(nz):
                r, c = i // per_q, q * per_q + i % per_q
                tile = h_xg[s, (my_x + nx - q) % nx, z_place(i)]
                hub_acc[8 * r : 8 * r + 8, 128 * c : 128 * c + 128] = tile
        hub_in[...] = stacked(hub_acc[...])

    hub_start(0)
    both_sides(ext_copy, THERE[0])
    tiles_load.wait()

    def split_tiles(b):
        both = [split(tiles_f32[b, k]) for k in range(slots)]
        cat_hi[b] = jnp.concatenate([one[0] for one in both], axis=1)
        cat_lo[b] = jnp.concatenate([one[1] for one in both], axis=1)

    loop(0, nb, split_tiles)
    hub_z(0)
    both_sides(ext_copy, THERE[1])
    loop(1, nf, lambda k: cot_copy(k).start())

    entries = nb * slots
    none = 3 * nb
    row = lax.broadcasted_iota(jnp.int32, (slots, nb), 0)
    lane = lax.broadcasted_iota(jnp.int32, (slots, nb), 1)
    place = lane * slots + row
    counts = jnp.zeros((slots, nb), jnp.int32)
    for b in range(nb):
        counts = jnp.where(lane == b, count[b], counts)
    target = jnp.where(row < counts, cols_v[...], none)
    along = lax.broadcasted_iota(jnp.int32, (1, 128), 1)

    def one(flag):
        return jnp.where(flag, 1, 0)

    def rank_step(e, carry):
        rank, again, upto, found = carry
        b, k = e // slots, e % slots
        goal = jnp.where(k < count[b], cols[k, b], none)
        tie = one(target == goal) * one(place > e)
        return (
            rank + one(target > goal) + tie, jnp.maximum(again, tie),
            upto + one(along >= goal), jnp.maximum(found, one(along == goal)),
        )

    zero, zeros = jnp.zeros((slots, nb), jnp.int32), jnp.zeros((1, 128), jnp.int32)
    rank, again, upto, found = lax.fori_loop(0, entries, rank_step, (zero, zero, zeros, zeros))
    which, same = zeros, zeros
    for e in range(entries):
        b, k = e // slots, e % slots
        here = rank[k : k + 1, b : b + 1] == along
        which = jnp.where(here, e, which)
        same = jnp.where(here, again[k : k + 1, b : b + 1], same)
    order_v[0:1] = which
    order_v[1:2] = same
    order_v[2:3] = jnp.maximum(upto - 1, 0)
    order_v[3:4] = found
    order_copy = pltpu.make_async_copy(order_v, order, s_misc.at[2])
    order_copy.start()

    w_load.wait()
    w_st[...] = stacked(w_f32[...])
    wt_st[...] = stacked(w_f32[...].T)

    def split_adj(p):
        high, low = split(adj_f32[p])
        adj_hi[p] = high
        adj_lo[p] = low

    wait_for(adj_f32, s_adj)
    loop(0, nf // 2, split_adj)
    hub_zg(0)
    both_sides(ext_copy, THERE[2])
    loop(nf // 2, nf, split_adj)
    order_copy.wait()
    for h in reversed(range(len(pieces))):
        hub_xg(0, h)

    wait_for(ext.at[pl.ds(0, 2 * nb)], s_nbr.at[1])

    def tile_part(p):
        for j in range(pb):
            b = p * pb + j
            left = jnp.concatenate(
                [ext[cols[k, b]] * jnp.where(k < count[b], 1.0, 0.0) for k in range(slots)],
                axis=1,
            )
            y_send[j, p] = mm3(stacked(left), cat_hi[b], cat_lo[b], NT)

    loop(0, nf, tile_part)
    hub_end(0)

    def rows_of(p):
        return pl.ds(pl.multiple_of(fl * p, 8), fl)

    def y_copy(j, k):
        return remote(
            y_send.at[j, feat_peer(k)], y_all.at[j, rows_of(me)], s_y.at[j, 0], s_y.at[j, 1],
            f_dev(k),
        )

    def feat_order(i):
        return nf // 2 if nf < 4 else (nf // 2 + (1 - 2 * (i % 2)) * ((i + 1) // 2)) % nf

    def to_feats(copies, j):
        loop(0, nf - 1, lambda i: copies(j, feat_order(i)).start())

    def hub_part(i):
        k = feat_order(i)
        p = feat_peer(k)
        part = mm3(hub_in[...], adj_hi[p], adj_lo[p], NN)
        for j in range(pb):
            y_send[j, p] += part[:, 128 * j : 128 * j + 128]
        y_copy(0, k).start()

    loop(0, nf - 1, hub_part)
    for j in range(1, pb):
        to_feats(y_copy, j)
    part = mm3(hub_in[...], adj_hi[me], adj_lo[me], NN)
    for j in range(pb):
        y_all[j, rows_of(me)] = y_send[j, me] + part[:, 128 * j : 128 * j + 128]

    cot_own.wait()

    others = pl.ds(0, fl * (nf - 1))
    wait_for(cot_all.at[others, :], s_cot.at[1])

    def q_copy(j, k):
        at = q_all.at[me, :, pl.ds(128 * j, 128)]
        src = q_send.at[j, rows_of(feat_peer(k))]
        return remote(src, at, s_q.at[0], s_q.at[k], f_dev(k))

    y_parts, g_parts = [], []
    for j in range(pb):
        cols_j = slice(128 * j, 128 * j + 128)
        wait_for(y_all.at[j, others], s_y.at[j, 1])
        y_hi, y_lo = split(y_all[j])
        agg = mm3(wt_st[...], y_hi, y_lo, NN)
        sig = 1.0 / (1.0 + jnp.exp(-agg))
        act_send[:, cols_j] = agg * sig
        grad = cot_all[:, cols_j] * sig * (1.0 + agg * (1.0 - sig))
        g_hi, g_lo = split(grad)
        q_send[j] = mm3(w_st[...], g_hi, g_lo, NN)
        to_feats(q_copy, j)
        q_all[me, :, cols_j] = q_send[j, rows_of(me)]
        y_parts.append((y_hi, y_lo))
        g_parts.append(jnp.concatenate([g_hi, g_lo], axis=0))

    g_st = jnp.concatenate(g_parts, axis=1)
    y_hi, y_lo = [jnp.concatenate(one_part, axis=1) for one_part in zip(*y_parts)]
    terms = mm3(g_st, y_hi, y_lo, NT)
    for p in range(nf):
        wg_src[p % 2, p // 2] = terms[fl * p : fl * p + fl]
    pair = remote(wg_src.at[1 - my_core], wg_pair, s_wp.at[0], s_wp.at[1], to(dom, me + 1 - 2 * my_core))
    pair.start()

    def wf_copy(k):
        y = (my_y + k) % ny
        return remote(wg_half.at[y], wg_recv.at[k - 1], s_wf.at[0], s_wf.at[1], to(dom, y * 2 + my_core))

    def act_at(p):
        return act.at[:, pl.ds(pl.multiple_of(vw * p, 128), vw)]

    def act_copy(k):
        return remote(act_send.at[rows_of(feat_peer(k)), :], act_at(me), s_act.at[0], s_act.at[1], f_dev(k))

    act_own = pltpu.make_async_copy(act_send.at[rows_of(me), :], act_at(me), s_misc.at[3])
    act_own.start()

    def hub_back(p):
        left = stacked(q_all[p])
        return mm3(left, adj_hi[p], adj_lo[p], NT)

    hub_acc[...] = hub_back(me)

    def hub_step(k):
        wait_for(q_all.at[feat_from(k)], s_q.at[k])
        hub_acc[...] += hub_back(feat_from(k))

    loop(1, nf, hub_step)
    hub_start(1)
    pair.wait_recv()
    wg_half[...] = wg_src[my_core] + wg_pair[...]
    for k in [2, 1, 3] if ny > 2 else []:
        wf_copy(k).start()

    def slot_terms(p):
        for j in range(pb):
            b = p * pb + j
            left = stacked(q_all[p, :, 128 * j : 128 * j + 128])
            out = mm3(left, cat_hi[b], cat_lo[b], NN)
            for k in range(slots):
                contrib[b * slots + k] = out[:, 128 * k : 128 * k + 128]

    loop(0, nf, slot_terms)

    def run_step(j, total):
        total = total * order[1, j].astype(F32) + contrib[order[0, j]]
        runs[j] = total
        return total

    lax.fori_loop(0, nb * slots, run_step, jnp.zeros((fl, 128), F32))

    def summed(block):
        return runs[order[2, block]] * order[3, block].astype(F32)

    def back_send(b):
        b_send[0, b] = summed(b)
        b_send[1, b] = summed(2 * nb + b)

    loop(0, nb, back_send)

    def back_copy(side, h):
        at = pl.ds(quarter * h, quarter)
        device = (to(prv, me), to(nxt, me))[side]
        return remote(b_send.at[side, at], b_recv.at[side, at], s_back.at[0], s_back.at[1], device)

    both_sides(back_copy, BACK[0])
    hub_z(1)
    both_sides(back_copy, BACK[1])

    term = wg_half[my_y]
    if ny > 1:
        wait_for(wg_recv, s_wf.at[1])
    for k in range(1, ny):
        term += wg_recv[k - 1]
    part = full // nx
    for q in range(nx):
        wg_xsrc[q] = term[:, part * q : part * q + part]

    def wx_copy(k):
        return remote(wg_xsrc.at[x_peer(k)], wg_rx.at[k - 1], s_wx.at[0], s_wx.at[1], x_dev(k))

    for k in range(1, nx):
        wx_copy(k).start()

    hub_zg(1)
    both_sides(back_copy, BACK[2])
    loop(0, nf - 1, lambda i: act_copy(feat_order(i)).start())

    wait_for(wg_rx, s_wx.at[1])
    term = wg_xsrc[my_x]
    for k in range(1, nx):
        term += wg_rx[k - 1]
    term = term.T
    lanes = wg_zsrc.shape[2]
    if lanes > fl:
        term = jnp.concatenate([term, jnp.zeros((part, lanes - fl), F32)], axis=1)
    wg_zsrc[...] = term.reshape(wg_zsrc.shape)

    def wz_copy(k):
        return remote(wg_zsrc.at[z_peer(k)], wg_rz.at[k - 1], s_wz.at[0], s_wz.at[1], z_dev(k))

    loop(1, nz, lambda k: wz_copy(k).start())

    for h in reversed(range(len(pieces))):
        hub_xg(1, h)


    hub_end(1)
    wait_for(b_recv, s_back.at[1])

    def out_copy(p):
        return pltpu.make_async_copy(
            fg_out.at[p], fg.at[:, pl.ds(pl.multiple_of(vw * p, 128), vw)], s_out
        )

    def finish(p):
        both = mm(hub_in[...], pick[p], NT)
        placed = both[:fl] + both[fl:]
        for j in range(pb):
            b = p * pb + j
            own = summed(nb + b)
            total = placed[:, 128 * j : 128 * j + 128] + own + b_recv[0, b] + b_recv[1, b]
            fg_out[p, :, 128 * j : 128 * j + 128] = total
        out_copy(p).start()

    loop(0, nf, finish)

    wait_for(wg_rz, s_wz.at[1])
    term = wg_zsrc[my_z]
    for k in range(1, nz):
        term += wg_rz[k - 1]
    wg[...] = term[:, :fl] * (1.0 / math.sqrt(vl * nd))

    act_own.wait()
    wait_for(act.at[:, pl.ds(0, vw * (nf - 1))], s_act.at[1])
    pair.wait_send()
    wait_for(ext.at[pl.ds(0, 2 * nb)], s_nbr.at[0])
    wait_for(b_send, s_back.at[0])
    wait_for(cot_all.at[others, :], s_cot.at[0])
    for j in range(pb):
        wait_for(y_all.at[j, others], s_y.at[j, 0])
    wait_for(q_all.at[pl.ds(0, nf - 1)], s_q.at[0])
    wait_for(act_send.at[others, :], s_act.at[0])
    if ny > 1:
        wait_for(wg_recv, s_wf.at[0])
    wait_for(wg_rx, s_wx.at[0])
    wait_for(wg_rz, s_wz.at[0])
    for s in range(2):
        wait_for(h_rx.at[s], s_hx.at[s, 3])
        wait_for(h_rz.at[s], s_hz.at[s, 0])
        wait_for(h_rz.at[s], s_hzg.at[s, 3])
        wait_for(h_xg.at[s, pl.ds(1, nx - 1)], s_hxg.at[s, 0])
    wait_for(fg_out, s_out)


def hand_over_kernel(count, *refs):
    ins, outs = refs[:count], refs[count : 2 * count]
    held, sems = refs[2 * count : 3 * count], refs[-1]
    reads = [pltpu.make_async_copy(ins[i], held[i], sems.at[0, i]) for i in range(count)]
    writes = [pltpu.make_async_copy(held[i], outs[i], sems.at[1, i]) for i in range(count)]
    for read in reads:
        read.start()
    for read, write in zip(reads, writes):
        read.wait()
        write.start()
    for write in writes:
        write.wait()


def hand_over(arrays):
    hbm = pl.BlockSpec(memory_space=pl.ANY)
    count = len(arrays)
    return pl.pallas_call(
        functools.partial(hand_over_kernel, count),
        out_shape=tuple(jax.ShapeDtypeStruct(a.shape, a.dtype) for a in arrays),
        in_specs=[hbm] * count,
        out_specs=(hbm,) * count,
        scratch_shapes=[pltpu.VMEM(a.shape, a.dtype) for a in arrays]
        + [pltpu.SemaphoreType.DMA((2, count))],
        compiler_params=pltpu.CompilerParams(vmem_limit_bytes=60 * 1024 * 1024),
    )(*arrays)


def local(nd, nf, nx, node_feats, weight, tiles, block_cols, block_count, hub_ids, hub_adj, cotangent):
    nz = nd // nx
    fl, vl = node_feats.shape
    full = weight.shape[0]
    nb, slots = block_cols.shape
    nh = hub_adj.shape[0]
    vw = vl // nf
    entries = nb * slots
    ny, pb = nf // 2, nb // nf
    lanes = max(fl, 128)
    vm = pltpu.VMEM
    dma = pltpu.SemaphoreType.DMA
    hub_tile = (8, 128)
    scratch = [
        vm((3 * nb, fl, 128), F32),
        vm((nf, nh, vw), F32), vm((nf, nh, vw), BF16), vm((nf, nh, vw), BF16),
        vm((nb, slots, 128, 128), F32),
        vm((nb, 128, slots * 128), BF16), vm((nb, 128, slots * 128), BF16),
        vm((nf, vw, nh), BF16),
        vm((full, full), F32), vm((2 * full, full), BF16), vm((2 * full, full), BF16),
        vm((pb, nf, fl, 128), F32), vm((pb, full, 128), F32), vm((full, vw), F32),
        vm((full, vw), F32), vm((pb, full, 128), F32), vm((nf, fl, vw), F32),
        vm((fl, nh), F32), vm((2 * fl, nh), BF16),
        vm((entries, fl, 128), F32), vm((entries, fl, 128), F32),
        vm((2, nb, fl, 128), F32), vm((2, nb, fl, 128), F32), vm((nf, fl, vw), F32),
        vm((8, 128), jnp.int32), pltpu.SMEM((8, 128), jnp.int32),
        vm((2, nx, nz) + hub_tile, F32), vm((2, nx - 1, nz) + hub_tile, F32),
        vm((2, nz) + hub_tile, F32), vm((2, nz - 1) + hub_tile, F32),
        vm((2, nz) + hub_tile, F32), vm((2, nx, nz) + hub_tile, F32),
        vm((2, ny, fl, full), F32), vm((ny, fl, full), F32), vm((ny, fl, full), F32),
        vm((max(ny - 1, 1), fl, full), F32),
        vm((nx, fl, full // nx), F32), vm((nx - 1, fl, full // nx), F32),
        vm((nz, full // nx // nz, lanes), F32), vm((nz - 1, full // nx // nz, lanes), F32),
        dma, dma((4,)), dma, dma, dma,
        dma((2,)), dma((2,)), dma((pb, 2)), dma((nf,)), dma((2,)), dma((2,)),
        dma((2, 4)), dma((2, 2)), dma((2, 4)), dma((2, 2)),
        dma((2,)), dma((2,)), dma((2,)), dma((2,)),
    ]
    hbm = pl.BlockSpec(memory_space=pl.ANY)
    vmem = pl.BlockSpec(memory_space=pltpu.VMEM)
    smem = pl.BlockSpec(memory_space=pltpu.SMEM)
    results = pl.pallas_call(
        functools.partial(kernel, (nx, nz, nf, nb, slots)),
        out_shape=(
            jax.ShapeDtypeStruct((fl, vl), F32),
            jax.ShapeDtypeStruct((fl, vl), F32),
            jax.ShapeDtypeStruct((full // nd, fl), F32),
        ),
        in_specs=[hbm] * 5 + [vmem] * 2 + [smem] * 2,
        out_specs=(hbm, hbm, vmem),
        scratch_shapes=scratch,
        compiler_params=pltpu.CompilerParams(
            collective_id=0, has_side_effects=True, vmem_limit_bytes=60 * 1024 * 1024
        ),
    )(
        node_feats, weight, tiles, hub_adj, cotangent, hub_ids.reshape(nh // 128, 128),
        block_cols.T, block_cols.T, block_count,
    )
    return hand_over(results)


def solution(mesh):
    nd, nf = mesh.shape["dom"], mesh.shape["feat"]
    nx = 4 if nd == 64 else 2
    return jax.shard_map(
        functools.partial(local, nd, nf, nx),
        mesh=mesh,
        in_specs=(
            P("feat", "dom"),
            P(),
            P("dom", None, None, None),
            P("dom", None),
            P("dom"),
            P(),
            P(None, "dom"),
            P("feat", "dom"),
        ),
        out_specs=(P("feat", "dom"), P("feat", "dom"), P("dom", "feat")),
        check_vma=False,
    )
```

```python
import functools
import math

import jax
import jax.numpy as jnp
from jax import lax
from jax.experimental import pallas as pl
from jax.experimental.pallas import tpu as pltpu
from jax.sharding import PartitionSpec as P

MESH = pl.DeviceIdType.MESH
F32 = jnp.float32
BF16 = jnp.bfloat16
NN = (((1,), (0,)), ((), ()))
NT = (((1,), (1,)), ((), ()))
THERE = ((), (0, 1), (2, 3))
BACK = ((), (0, 1), (2, 3))


def split(value):
    high = value.astype(BF16)
    low = (value - high.astype(F32)).astype(BF16)
    return high, low


def mm(a, b, dims):
    return lax.dot_general(a, b, dims, preferred_element_type=F32)


def stacked(value):
    high, low = split(value)
    return jnp.concatenate([high, low], axis=0)


def mm3(left, right_high, right_low, dims):
    rows = left.shape[0] // 2
    both = mm(left, right_high, dims)
    return both[:rows] + both[rows:] + mm(left[:rows], right_low, dims)


def kernel(
    sizes,
    x, w, tiles, hub_adj, cot, ids_at, cols_at, count_at,
    act, fg, wg,
    ids, cols_v, cols, count, ext, adj_f32, adj_hi, adj_lo, tiles_f32, cat_hi, cat_lo, pick,
    w_f32, w_st, wt_st, y_send, y_all, cot_all, act_send, q_send, q_all,
    hub_acc, hub_in, contrib, runs, b_send, b_recv, fg_out, order_v, order,
    h_src, h_rx, h_zsrc, h_rz, h_zg, h_xg,
    wg_src, wg_pair, wg_half, wg_recv, wg_xsrc, wg_rx, wg_zsrc, wg_rz,
    s_small, s_x, s_misc, s_adj, s_cot_own, s_out,
    s_nbr, s_cot, s_y, s_q, s_act, s_back, s_hx, s_hz, s_hzg, s_hxg, s_wp, s_wf, s_wx, s_wz,
):
    nx, nz, nf, nb, slots = sizes
    ny = nf // 2
    nd = nx * nz
    fl, vl = x.shape
    full = w.shape[0]
    nh = hub_adj.shape[0]
    pb = nb // nf
    vw = pb * 128
    row_tiles = fl // 8
    per_q = nh // 128 // nx
    dom = lax.axis_index("dom")
    me = lax.axis_index("feat")
    my_x, my_z = dom // nz, dom % nz
    my_y, my_core = me // 2, me % 2
    nxt, prv = (dom + 1) % nd, (dom + nd - 1) % nd

    def feat_peer(k):
        return (me + k) % nf

    def feat_from(k):
        return (me + nf - k) % nf

    def x_peer(k):
        return (my_x + k) % nx

    def z_peer(k):
        return (my_z + k) % nz

    def z_step(o):
        return (nz // 2 + (1 - 2 * (o % 2)) * ((o + 1) // 2) + nz) % nz

    def z_back(o):
        return o + (2 * (o % 2) - 1) * ((o + nz - 1) // nz)

    def to(domain, feature):
        return {"dom": domain, "feat": feature}

    def x_dev(k):
        return to(x_peer(k) * nz + my_z, me)

    def z_dev(k):
        return to(my_x * nz + z_peer(k), me)

    def f_dev(k):
        return to(dom, feat_peer(k))

    def remote(src, dst, sent, came, device):
        return pltpu.make_async_remote_copy(
            src_ref=src, dst_ref=dst, send_sem=sent, recv_sem=came,
            device_id=device, device_id_type=MESH,
        )

    def wait_for(ref, sem):
        pltpu.make_async_copy(ref, ref, sem).wait()

    def loop(lower, upper, body):
        def step(i, carry):
            body(i)
            return carry

        lax.fori_loop(lower, upper, step, 0)

    barrier = pltpu.get_barrier_semaphore()

    def greet(device):
        pl.semaphore_signal(barrier, inc=1, device_id=device, device_id_type=MESH)

    loop(0, nz - 1, lambda o: greet(z_dev(z_step(o))))
    for k in range(1, nx):
        greet(x_dev(k))
    greet(to(nxt, me))
    greet(to(prv, me))
    loop(1, nf, lambda k: greet(f_dev(k)))
    small = [
        pltpu.make_async_copy(ids_at, ids, s_small.at[0]),
        pltpu.make_async_copy(cols_at, cols_v, s_small.at[1]),
        pltpu.make_async_copy(cols_at, cols, s_small.at[2]),
        pltpu.make_async_copy(count_at, count, s_small.at[3]),
    ]
    for copy in small:
        copy.start()
    x_loads = [
        pltpu.make_async_copy(x.at[:, pl.ds(128 * b, 128)], ext.at[nb + b], s_x)
        for b in range(nb)
    ]
    for copy in x_loads:
        copy.start()
    tiles_load = pltpu.make_async_copy(tiles, tiles_f32, s_misc.at[0])
    w_load = pltpu.make_async_copy(w, w_f32, s_misc.at[1])
    adj_loads = [
        pltpu.make_async_copy(hub_adj.at[:, pl.ds(vw * p, vw)], adj_f32.at[p], s_adj)
        for p in range(nf)
    ]
    cot_own = pltpu.make_async_copy(
        cot.at[:, pl.ds(pl.multiple_of(vw * me, 128), vw)],
        cot_all.at[pl.ds(pl.multiple_of(fl * me, 8), fl), :], s_cot_own,
    )
    tiles_load.start()
    w_load.start()
    cot_own.start()
    for copy in adj_loads:
        copy.start()


    quarter = nb // 4

    def ext_copy(side, h):
        at, device = ((0, to(nxt, me)), (2 * nb, to(prv, me)))[side]
        return remote(
            ext.at[pl.ds(nb + quarter * h, quarter)], ext.at[pl.ds(at + quarter * h, quarter)],
            s_nbr.at[0], s_nbr.at[1], device,
        )

    def both_sides(copies, which):
        for h in which:
            copies(0, h).start()
            copies(1, h).start()

    def cot_copy(k):
        p = feat_peer(k)
        return remote(
            cot.at[:, pl.ds(pl.multiple_of(vw * p, 128), vw)],
            cot_all.at[pl.ds(pl.multiple_of(fl * me, 8), fl), :], s_cot.at[0], s_cot.at[1],
            f_dev(k),
        )

    for copy in small:
        copy.wait()
    local_id = ids[...] - dom * vl
    hub_acc[...] = jnp.zeros_like(hub_acc)

    def select(p):
        row = lax.broadcasted_iota(jnp.int32, (vw, 128), 0) + p * vw
        pick[p] = jnp.concatenate(
            [
                jnp.where(row == local_id[g : g + 1], 1.0, 0.0).astype(BF16)
                for g in range(nh // 128)
            ],
            axis=1,
        )

    loop(0, nf, select)
    wait_for(ext.at[pl.ds(nb, nb)], s_x)

    def own_hubs(p):
        left = stacked(jnp.concatenate([ext[nb + pb * p + j] for j in range(pb)], axis=1))
        both = mm(left, pick[p], NN)
        hub_acc[...] += both[:fl] + both[fl:]

    loop(0, nf, own_hubs)

    pl.semaphore_wait(barrier, 2 + (nx - 1) + (nz - 1) + (nf - 1))

    cuts = (0, 3, 9, nz) if nz == 16 else (0, 1, nz)
    pieces = [(cuts[i], cuts[i + 1]) for i in range(len(cuts) - 1)]
    own_at = nz - 1

    def piece(h):
        lower, upper = pieces[h]
        return pl.ds(lower, upper - lower)

    def z_loop(h, body):
        lower, upper = pieces[h]
        loop(lower, min(upper, nz - 1), body)

    def x_rs_copy(s, k, h):
        at = piece(h)
        return remote(
            h_src.at[s, x_peer(k), at], h_rx.at[s, k - 1, at], s_hx.at[s, 3], s_hx.at[s, h],
            x_dev(k),
        )

    def z_rs_copy(s, o):
        sent, came = s_hz.at[s, 0], s_hz.at[s, 1]
        return remote(h_zsrc.at[s, o], h_rz.at[s, o], sent, came, z_dev(z_step(o)))

    def z_ag_copy(s, o, h):
        dst = h_zg.at[s, z_back(o)]
        return remote(h_zg.at[s, own_at], dst, s_hzg.at[s, 3], s_hzg.at[s, h], z_dev(z_step(o)))

    def x_ag_copy(s, k, h):
        at = piece(h)
        return remote(h_zg.at[s, at], h_xg.at[s, k, at], s_hxg.at[s, 0], s_hxg.at[s, 1], x_dev(k))

    x_order = [2, 1, 3][:nx] if nx > 2 else [1]

    def z_place(i):
        step = (i + nz - my_z) % nz
        down = 2 * (nz // 2 - step) - 1
        up = 2 * (step - nz // 2)
        return jnp.where(step < nz // 2, down, up)

    def hub_start(s):
        for q in range(nx):
            for i in range(nz):
                r, c = i // per_q, q * per_q + i % per_q
                h_src[s, q, z_place(i)] = hub_acc[8 * r : 8 * r + 8, 128 * c : 128 * c + 128]
        for h in range(len(pieces)):
            for k in x_order:
                x_rs_copy(s, k, h).start()

    def hub_z(s):
        for h in range(len(pieces)):
            at = piece(h)
            wait_for(h_rx.at[s, :, at], s_hx.at[s, h])
            total = h_src[s, my_x, at]
            for k in range(1, nx):
                total += h_rx[s, k - 1, at]
            h_zsrc[s, at] = total
            z_loop(h, lambda o: z_rs_copy(s, o).start())

    def hub_zg(s):
        wait_for(h_rz.at[s], s_hz.at[s, 1])
        total = h_zsrc[s, own_at]
        for o in range(nz - 1):
            total += h_rz[s, o]
        h_zg[s, own_at] = total
        for h in range(len(pieces)):
            z_loop(h, lambda o: z_ag_copy(s, o, h).start())

    def hub_xg(s, h):
        lower, upper = pieces[h]
        if min(upper, nz - 1) > lower:
            wait_for(h_zg.at[s, pl.ds(lower, min(upper, nz - 1) - lower)], s_hzg.at[s, h])
        for k in x_order:
            x_ag_copy(s, k, h).start()
        at = piece(h)
        h_xg[s, 0, at] = h_zg[s, at]

    def hub_end(s):
        wait_for(h_xg.at[s, pl.ds(1, nx - 1)], s_hxg.at[s, 1])
        for q in range(nx):
            for i in range(nz):
                r, c = i // per_q, q * per_q + i % per_q
                tile = h_xg[s, (my_x + nx - q) % nx, z_place(i)]
                hub_acc[8 * r : 8 * r + 8, 128 * c : 128 * c + 128] = tile
        hub_in[...] = stacked(hub_acc[...])

    hub_start(0)
    both_sides(ext_copy, THERE[0])
    tiles_load.wait()

    def split_tiles(b):
        both = [split(tiles_f32[b, k]) for k in range(slots)]
        cat_hi[b] = jnp.concatenate([one[0] for one in both], axis=1)
        cat_lo[b] = jnp.concatenate([one[1] for one in both], axis=1)

    loop(0, nb, split_tiles)
    hub_z(0)
    both_sides(ext_copy, THERE[1])
    loop(1, nf, lambda k: cot_copy(k).start())

    entries = nb * slots
    none = 3 * nb
    row = lax.broadcasted_iota(jnp.int32, (slots, nb), 0)
    lane = lax.broadcasted_iota(jnp.int32, (slots, nb), 1)
    place = lane * slots + row
    counts = jnp.zeros((slots, nb), jnp.int32)
    for b in range(nb):
        counts = jnp.where(lane == b, count[b], counts)
    target = jnp.where(row < counts, cols_v[...], none)
    along = lax.broadcasted_iota(jnp.int32, (1, 128), 1)

    def one(flag):
        return jnp.where(flag, 1, 0)

    def rank_step(e, carry):
        rank, again, upto, found = carry
        b, k = e // slots, e % slots
        goal = jnp.where(k < count[b], cols[k, b], none)
        tie = one(target == goal) * one(place > e)
        return (
            rank + one(target > goal) + tie, jnp.maximum(again, tie),
            upto + one(along >= goal), jnp.maximum(found, one(along == goal)),
        )

    zero, zeros = jnp.zeros((slots, nb), jnp.int32), jnp.zeros((1, 128), jnp.int32)
    rank, again, upto, found = lax.fori_loop(0, entries, rank_step, (zero, zero, zeros, zeros))
    which, same = zeros, zeros
    for e in range(entries):
        b, k = e // slots, e % slots
        here = rank[k : k + 1, b : b + 1] == along
        which = jnp.where(here, e, which)
        same = jnp.where(here, again[k : k + 1, b : b + 1], same)
    order_v[0:1] = which
    order_v[1:2] = same
    order_v[2:3] = jnp.maximum(upto - 1, 0)
    order_v[3:4] = found
    order_copy = pltpu.make_async_copy(order_v, order, s_misc.at[2])
    order_copy.start()

    w_load.wait()
    w_st[...] = stacked(w_f32[...])
    wt_st[...] = stacked(w_f32[...].T)

    def split_adj(p):
        high, low = split(adj_f32[p])
        adj_hi[p] = high
        adj_lo[p] = low

    wait_for(adj_f32, s_adj)
    loop(0, nf // 2, split_adj)
    hub_zg(0)
    both_sides(ext_copy, THERE[2])
    loop(nf // 2, nf, split_adj)
    order_copy.wait()
    for h in reversed(range(len(pieces))):
        hub_xg(0, h)

    wait_for(ext.at[pl.ds(0, 2 * nb)], s_nbr.at[1])

    def tile_part(p):
        for j in range(pb):
            b = p * pb + j
            left = jnp.concatenate(
                [ext[cols[k, b]] * jnp.where(k < count[b], 1.0, 0.0) for k in range(slots)],
                axis=1,
            )
            y_send[j, p] = mm3(stacked(left), cat_hi[b], cat_lo[b], NT)

    loop(0, nf, tile_part)
    hub_end(0)

    def rows_of(p):
        return pl.ds(pl.multiple_of(fl * p, 8), fl)

    def y_copy(j, k):
        return remote(
            y_send.at[j, feat_peer(k)], y_all.at[j, rows_of(me)], s_y.at[j, 0], s_y.at[j, 1],
            f_dev(k),
        )

    def feat_order(i):
        return nf // 2 if nf < 4 else (nf // 2 + (1 - 2 * (i % 2)) * ((i + 1) // 2)) % nf

    def to_feats(copies, j):
        loop(0, nf - 1, lambda i: copies(j, feat_order(i)).start())

    def hub_part(i):
        k = feat_order(i)
        p = feat_peer(k)
        part = mm3(hub_in[...], adj_hi[p], adj_lo[p], NN)
        for j in range(pb):
            y_send[j, p] += part[:, 128 * j : 128 * j + 128]
        y_copy(0, k).start()

    loop(0, nf - 1, hub_part)
    for j in range(1, pb):
        to_feats(y_copy, j)
    part = mm3(hub_in[...], adj_hi[me], adj_lo[me], NN)
    for j in range(pb):
        y_all[j, rows_of(me)] = y_send[j, me] + part[:, 128 * j : 128 * j + 128]

    cot_own.wait()

    others = pl.ds(0, fl * (nf - 1))
    wait_for(cot_all.at[others, :], s_cot.at[1])

    def q_copy(j, k):
        at = q_all.at[me, :, pl.ds(128 * j, 128)]
        src = q_send.at[j, rows_of(feat_peer(k))]
        return remote(src, at, s_q.at[0], s_q.at[k], f_dev(k))

    y_parts, g_parts = [], []
    for j in range(pb):
        cols_j = slice(128 * j, 128 * j + 128)
        wait_for(y_all.at[j, others], s_y.at[j, 1])
        y_hi, y_lo = split(y_all[j])
        agg = mm3(wt_st[...], y_hi, y_lo, NN)
        sig = 1.0 / (1.0 + jnp.exp(-agg))
        act_send[:, cols_j] = agg * sig
        grad = cot_all[:, cols_j] * sig * (1.0 + agg * (1.0 - sig))
        g_hi, g_lo = split(grad)
        q_send[j] = mm3(w_st[...], g_hi, g_lo, NN)
        to_feats(q_copy, j)
        q_all[me, :, cols_j] = q_send[j, rows_of(me)]
        y_parts.append((y_hi, y_lo))
        g_parts.append(jnp.concatenate([g_hi, g_lo], axis=0))

    g_st = jnp.concatenate(g_parts, axis=1)
    y_hi, y_lo = [jnp.concatenate(one_part, axis=1) for one_part in zip(*y_parts)]
    terms = mm3(g_st, y_hi, y_lo, NT)
    for p in range(nf):
        wg_src[p % 2, p // 2] = terms[fl * p : fl * p + fl]
    pair = remote(wg_src.at[1 - my_core], wg_pair, s_wp.at[0], s_wp.at[1], to(dom, me + 1 - 2 * my_core))
    pair.start()

    def wf_copy(k):
        y = (my_y + k) % ny
        return remote(wg_half.at[y], wg_recv.at[k - 1], s_wf.at[0], s_wf.at[1], to(dom, y * 2 + my_core))

    def act_at(p):
        return act.at[:, pl.ds(pl.multiple_of(vw * p, 128), vw)]

    def act_copy(k):
        return remote(act_send.at[rows_of(feat_peer(k)), :], act_at(me), s_act.at[0], s_act.at[1], f_dev(k))

    act_own = pltpu.make_async_copy(act_send.at[rows_of(me), :], act_at(me), s_misc.at[3])
    act_own.start()

    def hub_back(p):
        left = stacked(q_all[p])
        return mm3(left, adj_hi[p], adj_lo[p], NT)

    hub_acc[...] = hub_back(me)

    def hub_step(k):
        wait_for(q_all.at[feat_from(k)], s_q.at[k])
        hub_acc[...] += hub_back(feat_from(k))

    loop(1, nf, hub_step)
    hub_start(1)
    pair.wait_recv()
    wg_half[...] = wg_src[my_core] + wg_pair[...]
    for k in [2, 1, 3] if ny > 2 else []:
        wf_copy(k).start()

    def slot_terms(p):
        for j in range(pb):
            b = p * pb + j
            left = stacked(q_all[p, :, 128 * j : 128 * j + 128])
            out = mm3(left, cat_hi[b], cat_lo[b], NN)
            for k in range(slots):
                contrib[b * slots + k] = out[:, 128 * k : 128 * k + 128]

    loop(0, nf, slot_terms)

    def run_step(j, total):
        total = total * order[1, j].astype(F32) + contrib[order[0, j]]
        runs[j] = total
        return total

    lax.fori_loop(0, nb * slots, run_step, jnp.zeros((fl, 128), F32))

    def summed(block):
        return runs[order[2, block]] * order[3, block].astype(F32)

    def back_send(b):
        b_send[0, b] = summed(b)
        b_send[1, b] = summed(2 * nb + b)

    loop(0, nb, back_send)

    def back_copy(side, h):
        at = pl.ds(quarter * h, quarter)
        device = (to(prv, me), to(nxt, me))[side]
        return remote(b_send.at[side, at], b_recv.at[side, at], s_back.at[0], s_back.at[1], device)

    both_sides(back_copy, BACK[0])
    hub_z(1)
    both_sides(back_copy, BACK[1])

    term = wg_half[my_y]
    if ny > 1:
        wait_for(wg_recv, s_wf.at[1])
    for k in range(1, ny):
        term += wg_recv[k - 1]
    part = full // nx
    for q in range(nx):
        wg_xsrc[q] = term[:, part * q : part * q + part]

    def wx_copy(k):
        return remote(wg_xsrc.at[x_peer(k)], wg_rx.at[k - 1], s_wx.at[0], s_wx.at[1], x_dev(k))

    for k in range(1, nx):
        wx_copy(k).start()

    hub_zg(1)
    both_sides(back_copy, BACK[2])
    loop(0, nf - 1, lambda i: act_copy(feat_order(i)).start())

    wait_for(wg_rx, s_wx.at[1])
    term = wg_xsrc[my_x]
    for k in range(1, nx):
        term += wg_rx[k - 1]
    term = term.T
    lanes = wg_zsrc.shape[2]
    if lanes > fl:
        term = jnp.concatenate([term, jnp.zeros((part, lanes - fl), F32)], axis=1)
    wg_zsrc[...] = term.reshape(wg_zsrc.shape)

    def wz_copy(k):
        return remote(wg_zsrc.at[z_peer(k)], wg_rz.at[k - 1], s_wz.at[0], s_wz.at[1], z_dev(k))

    loop(1, nz, lambda k: wz_copy(k).start())

    for h in reversed(range(len(pieces))):
        hub_xg(1, h)


    wait_for(b_recv, s_back.at[1])

    def near_sum(p):
        for j in range(pb):
            b = p * pb + j
            fg_out[p, :, 128 * j : 128 * j + 128] = summed(nb + b) + b_recv[0, b] + b_recv[1, b]

    loop(0, nf, near_sum)
    hub_end(1)

    def out_copy(p):
        return pltpu.make_async_copy(
            fg_out.at[p], fg.at[:, pl.ds(pl.multiple_of(vw * p, 128), vw)], s_out
        )

    def finish(p):
        both = mm(hub_in[...], pick[p], NT)
        fg_out[p] += both[:fl] + both[fl:]
        out_copy(p).start()

    loop(0, nf, finish)

    wait_for(wg_rz, s_wz.at[1])
    term = wg_zsrc[my_z]
    for k in range(1, nz):
        term += wg_rz[k - 1]
    wg[...] = term[:, :fl] * (1.0 / math.sqrt(vl * nd))

    act_own.wait()
    wait_for(act.at[:, pl.ds(0, vw * (nf - 1))], s_act.at[1])
    pair.wait_send()
    wait_for(ext.at[pl.ds(0, 2 * nb)], s_nbr.at[0])
    wait_for(b_send, s_back.at[0])
    wait_for(cot_all.at[others, :], s_cot.at[0])
    for j in range(pb):
        wait_for(y_all.at[j, others], s_y.at[j, 0])
    wait_for(q_all.at[pl.ds(0, nf - 1)], s_q.at[0])
    wait_for(act_send.at[others, :], s_act.at[0])
    if ny > 1:
        wait_for(wg_recv, s_wf.at[0])
    wait_for(wg_rx, s_wx.at[0])
    wait_for(wg_rz, s_wz.at[0])
    for s in range(2):
        wait_for(h_rx.at[s], s_hx.at[s, 3])
        wait_for(h_rz.at[s], s_hz.at[s, 0])
        wait_for(h_rz.at[s], s_hzg.at[s, 3])
        wait_for(h_xg.at[s, pl.ds(1, nx - 1)], s_hxg.at[s, 0])
    wait_for(fg_out, s_out)


def hand_over_kernel(count, *refs):
    ins, outs = refs[:count], refs[count : 2 * count]
    held, sems = refs[2 * count : 3 * count], refs[-1]
    reads = [pltpu.make_async_copy(ins[i], held[i], sems.at[0, i]) for i in range(count)]
    writes = [pltpu.make_async_copy(held[i], outs[i], sems.at[1, i]) for i in range(count)]
    for read in reads:
        read.start()
    for read, write in zip(reads, writes):
        read.wait()
        write.start()
    for write in writes:
        write.wait()


def hand_over(arrays):
    hbm = pl.BlockSpec(memory_space=pl.ANY)
    count = len(arrays)
    return pl.pallas_call(
        functools.partial(hand_over_kernel, count),
        out_shape=tuple(jax.ShapeDtypeStruct(a.shape, a.dtype) for a in arrays),
        in_specs=[hbm] * count,
        out_specs=(hbm,) * count,
        scratch_shapes=[pltpu.VMEM(a.shape, a.dtype) for a in arrays]
        + [pltpu.SemaphoreType.DMA((2, count))],
        compiler_params=pltpu.CompilerParams(vmem_limit_bytes=60 * 1024 * 1024),
    )(*arrays)


def local(nd, nf, nx, node_feats, weight, tiles, block_cols, block_count, hub_ids, hub_adj, cotangent):
    nz = nd // nx
    fl, vl = node_feats.shape
    full = weight.shape[0]
    nb, slots = block_cols.shape
    nh = hub_adj.shape[0]
    vw = vl // nf
    entries = nb * slots
    ny, pb = nf // 2, nb // nf
    lanes = max(fl, 128)
    vm = pltpu.VMEM
    dma = pltpu.SemaphoreType.DMA
    hub_tile = (8, 128)
    scratch = [
        vm((nh // 128, 128), jnp.int32), vm((slots, nb), jnp.int32),
        pltpu.SMEM((slots, nb), jnp.int32), pltpu.SMEM((nb,), jnp.int32),
        vm((3 * nb, fl, 128), F32),
        vm((nf, nh, vw), F32), vm((nf, nh, vw), BF16), vm((nf, nh, vw), BF16),
        vm((nb, slots, 128, 128), F32),
        vm((nb, 128, slots * 128), BF16), vm((nb, 128, slots * 128), BF16),
        vm((nf, vw, nh), BF16),
        vm((full, full), F32), vm((2 * full, full), BF16), vm((2 * full, full), BF16),
        vm((pb, nf, fl, 128), F32), vm((pb, full, 128), F32), vm((full, vw), F32),
        vm((full, vw), F32), vm((pb, full, 128), F32), vm((nf, fl, vw), F32),
        vm((fl, nh), F32), vm((2 * fl, nh), BF16),
        vm((entries, fl, 128), F32), vm((entries, fl, 128), F32),
        vm((2, nb, fl, 128), F32), vm((2, nb, fl, 128), F32), vm((nf, fl, vw), F32),
        vm((8, 128), jnp.int32), pltpu.SMEM((8, 128), jnp.int32),
        vm((2, nx, nz) + hub_tile, F32), vm((2, nx - 1, nz) + hub_tile, F32),
        vm((2, nz) + hub_tile, F32), vm((2, nz - 1) + hub_tile, F32),
        vm((2, nz) + hub_tile, F32), vm((2, nx, nz) + hub_tile, F32),
        vm((2, ny, fl, full), F32), vm((ny, fl, full), F32), vm((ny, fl, full), F32),
        vm((max(ny - 1, 1), fl, full), F32),
        vm((nx, fl, full // nx), F32), vm((nx - 1, fl, full // nx), F32),
        vm((nz, full // nx // nz, lanes), F32), vm((nz - 1, full // nx // nz, lanes), F32),
        dma((4,)), dma, dma((4,)), dma, dma, dma,
        dma((2,)), dma((2,)), dma((pb, 2)), dma((nf,)), dma((2,)), dma((2,)),
        dma((2, 4)), dma((2, 2)), dma((2, 4)), dma((2, 2)),
        dma((2,)), dma((2,)), dma((2,)), dma((2,)),
    ]
    hbm = pl.BlockSpec(memory_space=pl.ANY)
    vmem = pl.BlockSpec(memory_space=pltpu.VMEM)
    results = pl.pallas_call(
        functools.partial(kernel, (nx, nz, nf, nb, slots)),
        out_shape=(
            jax.ShapeDtypeStruct((fl, vl), F32),
            jax.ShapeDtypeStruct((fl, vl), F32),
            jax.ShapeDtypeStruct((full // nd, fl), F32),
        ),
        in_specs=[hbm] * 8,
        out_specs=(hbm, hbm, vmem),
        scratch_shapes=scratch,
        compiler_params=pltpu.CompilerParams(
            collective_id=0, has_side_effects=True, vmem_limit_bytes=60 * 1024 * 1024
        ),
    )(
        node_feats, weight, tiles, hub_adj, cotangent, hub_ids.reshape(nh // 128, 128),
        block_cols.T, block_count,
    )
    return hand_over(results)


def solution(mesh):
    nd, nf = mesh.shape["dom"], mesh.shape["feat"]
    nx = 4 if nd == 64 else 2
    return jax.shard_map(
        functools.partial(local, nd, nf, nx),
        mesh=mesh,
        in_specs=(
            P("feat", "dom"),
            P(),
            P("dom", None, None, None),
            P("dom", None),
            P("dom"),
            P(),
            P(None, "dom"),
            P("feat", "dom"),
        ),
        out_specs=(P("feat", "dom"), P("feat", "dom"), P("dom", "feat")),
        check_vma=False,
    )
```
